32 devices in a mesh: outer: 4 (over y, x), inner: 8 (over z, core).
Axes of the slice: x: 2, y: 2, z: 4, core: 2. Of those that a mesh axis runs over, the one named last changes fastest.
Arguments:
- weights: float32 [16384, 128], P(('outer', 'inner')), may hold values from -1.5 to 1.5
Outputs:
- level_weights: float32 [16384, 128], P(('outer', 'inner'))
The draws below stay inside these ranges and needn't reach their ends.
All inputs are finite; a program needn't handle non-finite values.
Results may differ from the reference program's by a relative error of at most 0.0049.
Values sent between devices are 32-bit elements; how exact they have to be, the bound alone decides.
No kernel may reach another device: no remote copies, remote signals or barrier semaphores. Data moves between devices by JAX's collectives and lax.ppermute only.
A program may use at most 64 MiB of HBM per device.

```python
import jax
import jax.numpy as jnp
import numpy as np
from jax import lax

GRID_N = 16384
TREE_LEVELS = 11
PAIRS_DEV = 512
PAIRS = 16384
LEVELS = 5
N_OUTER = 4
N_INNER = 8


def level_of(rng, extent, cuts, smallest, high):
    gain = 1.0
    for dim, blocks in cuts:
        draws = jax.random.uniform(jax.random.fold_in(jax.random.fold_in(rng, 6), dim), (blocks,), jnp.float32, smallest / len(cuts), high / len(cuts))
        gain = gain * jnp.repeat(jnp.exp(draws), extent[dim] // blocks).reshape((-1,) + (1,) * (len(extent) - 1 - dim))
    return gain


def centred(stream_key, dims, spread, bound, split=(), kind=jnp.bfloat16):
    loudness = level_of(stream_key, dims, split, -0.22, 0.18) if split else 1.0
    result = jax.random.normal(stream_key, dims, jnp.float32) * spread * loudness
    return jnp.minimum(jnp.maximum(result, -bound), bound).astype(kind)


def setup_inputs(seed: int = 0) -> dict:
    streams_of = jax.random.split(jax.random.key(seed), 2)
    weights = centred(streams_of[0], (PAIRS, 128), (0.5 ** (LEVELS // 2)), 1.5, ((0, 32),), jnp.float32)
    return dict(weights=weights)


def chebyshev_nodes():
    return 0.5 * np.cos(np.pi * (2.0 * np.arange(8) + 1.0) / 16.0)

def lagrange_weights(which_child):
    node_values = chebyshev_nodes()
    targets = (node_values + which_child - 0.5) / 2.0
    weights_table = np.ones((8, 8))
    for anchor in range(8):
        for other_node in range(8):
            if other_node != anchor:
                weights_table[anchor, :] = weights_table[anchor, :] * (targets - node_values[other_node]) / (node_values[anchor] - node_values[other_node])
    return weights_table

def merge_matrix(dimension):
    merge_table = np.zeros((256, 128))
    for which_child in range(2):
        weights_table = lagrange_weights(which_child)
        if dimension == 0:
            block_table = np.kron(weights_table, np.eye(8))
        else:
            block_table = np.kron(np.eye(8), weights_table)
        for component in range(2):
            merge_table[which_child * 128 + component * 64:which_child * 128 + component * 64 + 64, component * 64:component * 64 + 64] = block_table.T
    return jnp.asarray(merge_table, dtype=jnp.float32)

def level_plan(local_bits, inner_bits, outer_bits):
    levels_total = inner_bits + outer_bits
    source_bits = [[], []]
    for level_number in range(levels_total):
        source_bits[(level_number + 1) % 2].append(local_bits + level_number)
    source_bits[0] = source_bits[0] + [local_bits - 7, local_bits - 6, local_bits - 5]
    source_bits[1] = source_bits[1] + [local_bits - 4, local_bits - 3, local_bits - 2, local_bits - 1]
    target_bits = [[], []]
    for ordinal in range(local_bits - 7):
        target_bits[ordinal % 2].append(ordinal)
    level_list = []
    for level_number in range(levels_total):
        dimension = (level_number + 1) % 2
        carried_bit = local_bits + level_number
        if level_number < inner_bits:
            moved_bit = local_bits - inner_bits + level_number
        else:
            moved_bit = local_bits - levels_total + level_number - inner_bits
        level_list.append((dimension, carried_bit, moved_bit, [list(bit_group) for bit_group in target_bits], [list(bit_group) for bit_group in source_bits]))
        target_bits = [[carried_bit if bit_place == moved_bit else bit_place for bit_place in bit_group] for bit_group in target_bits]
        source_bits = [[carried_bit if bit_place == moved_bit else bit_place for bit_place in bit_group] for bit_group in source_bits]
        source_bits[dimension] = source_bits[dimension][1:]
        target_bits[dimension] = [moved_bit] + target_bits[dimension]
    return level_list

def bit_value(row_index, positions):
    assembled = jnp.zeros_like(row_index)
    for ordinal, position in enumerate(positions):
        assembled = assembled + ((row_index >> position & 1) << ordinal)
    return assembled

def spread_grid(values, axis_place):
    row_count = values.shape[0]
    if axis_place == 0:
        shaped = values[:, None, :, None]
    else:
        shaped = values[:, None, None, :]
    return jnp.broadcast_to(shaped, (row_count, 2, 8, 8)).reshape(row_count, 128)

def dimension_terms(target_index, target_level, source_index, source_level):
    node_values = jnp.asarray(chebyshev_nodes(), dtype=jnp.float32)
    box_width = 2.0 ** (-source_level)
    center = (target_index.astype(jnp.float32) + 0.5) * (GRID_N * 2.0 ** (-target_level)) - GRID_N / 2.0
    offsets = node_values * box_width
    position = (source_index.astype(jnp.float32) + 0.5)[:, None] * box_width + offsets[None, :]
    linear = offsets[None, :] * center[:, None]
    return (center, position, linear)

def phase_cycles(target_index, target_level, source_index, source_level):
    center_one, place_one, linear_one = dimension_terms(target_index[0], target_level[0], source_index[0], source_level[0])
    center_two, place_two, linear_two = dimension_terms(target_index[1], target_level[1], source_index[1], source_level[1])
    turn = 2.0 * np.pi
    sine_one = spread_grid(jnp.sin(turn * place_one), 0)
    sine_two = spread_grid(jnp.sin(turn * place_two), 1)
    cosine_one = spread_grid(jnp.cos(turn * place_one), 0)
    cosine_two = spread_grid(jnp.cos(turn * place_two), 1)
    coeff_one = (2.0 + sine_one * sine_two) / 16.0
    coeff_two = (2.0 + cosine_one * cosine_two) / 16.0
    radial = jnp.sqrt((coeff_one * center_one[:, None]) ** 2 + (coeff_two * center_two[:, None]) ** 2)
    linear = spread_grid(linear_one, 0) + spread_grid(linear_two, 1)
    return linear - jnp.floor(linear) + (radial - jnp.floor(radial))

def rotate(values, cycles, direction):
    radians = 2.0 * np.pi * cycles
    cosine = jnp.cos(radians)
    sine_part = jnp.sin(radians) * direction
    swapped = jnp.concatenate([values[:, 64:], values[:, :64]], axis=1)
    sign_pattern = jnp.concatenate([-jnp.ones((64,), jnp.float32), jnp.ones((64,), jnp.float32)])
    return values * cosine + swapped * (sine_part * sign_pattern)

def combine(first_child, second_child, base_index, layout, merge_table):
    dimension, target_bits, source_bits = (layout[0], layout[3], layout[4])
    children = [first_child, second_child]
    target_index = [bit_value(base_index, target_bits[0]), bit_value(base_index, target_bits[1])]
    source_index = [bit_value(base_index, source_bits[0]), bit_value(base_index, source_bits[1])]
    source_level = [len(source_bits[0]), len(source_bits[1])]
    target_level = [TREE_LEVELS - source_level[0], TREE_LEVELS - source_level[1]]
    results = []
    for branch in range(2):
        new_target = list(target_index)
        new_target[dimension] = 2 * target_index[dimension] + branch
        new_level = list(target_level)
        new_level[dimension] = target_level[dimension] + 1
        rotated = []
        for which_child in range(2):
            child_source = list(source_index)
            child_source[dimension] = source_index[dimension] + which_child
            rotated.append(rotate(children[which_child], phase_cycles(new_target, new_level, child_source, source_level), 1.0))
        stacked = jnp.concatenate(rotated, axis=1)
        merged = jnp.dot(stacked, merge_table, precision=lax.Precision.HIGHEST, preferred_element_type=jnp.float32)
        parent_source = list(source_index)
        parent_source[dimension] = source_index[dimension] // 2
        parent_level = list(source_level)
        parent_level[dimension] = source_level[dimension] - 1
        results.append(rotate(merged, phase_cycles(new_target, new_level, parent_source, parent_level), -1.0))
    return results

def reference(weights):
    local_bits = PAIRS_DEV.bit_length() - 1
    inner_bits = N_INNER.bit_length() - 1
    outer_bits = N_OUTER.bit_length() - 1
    row_count = weights.shape[0]
    current = weights
    for layout in level_plan(local_bits, inner_bits, outer_bits):
        dimension, carried_bit, moved_bit = (layout[0], layout[1], layout[2])
        merge_table = merge_matrix(dimension)
        outer_count = row_count >> carried_bit + 1
        middle_count = 2 ** (carried_bit - moved_bit - 1)
        inner_count = 2 ** moved_bit
        shaped = current.reshape(outer_count, 2, middle_count, 2, inner_count, 128)
        indices = jnp.arange(row_count, dtype=jnp.int32).reshape(outer_count, 2, middle_count, 2, inner_count)[:, 0].reshape(-1)
        first_child = shaped[:, 0].reshape(-1, 128)
        second_child = shaped[:, 1].reshape(-1, 128)
        outputs = combine(first_child, second_child, indices, layout, merge_table)
        stacked = jnp.stack([branch_out.reshape(outer_count, middle_count, 2, inner_count, 128) for branch_out in outputs], axis=3)
        current = jnp.moveaxis(stacked, 2, 1).reshape(row_count, 128)
    return current
```

```python
import functools

import jax
import jax.numpy as jnp
import numpy as np
from jax import lax
from jax.experimental import pallas as pl
from jax.experimental.pallas import tpu as pltpu
from jax.sharding import PartitionSpec as P

GRID_N = 16384
TREE_LEVELS = 11
LOW_BITS = 4
BLOCK = 1 << LOW_BITS


def chebyshev_nodes():
    return 0.5 * np.cos(np.pi * (2.0 * np.arange(8) + 1.0) / 16.0)


def lagrange_weights(which_child):
    node_values = chebyshev_nodes()
    targets = (node_values + which_child - 0.5) / 2.0
    weights_table = np.ones((8, 8))
    for anchor in range(8):
        for other_node in range(8):
            if other_node != anchor:
                weights_table[anchor, :] = (
                    weights_table[anchor, :]
                    * (targets - node_values[other_node])
                    / (node_values[anchor] - node_values[other_node])
                )
    return weights_table


def merge_matrix(dimension):
    merge_table = np.zeros((256, 128))
    for which_child in range(2):
        weights_table = lagrange_weights(which_child)
        if dimension == 0:
            block_table = np.kron(weights_table, np.eye(8))
        else:
            block_table = np.kron(np.eye(8), weights_table)
        for half in range(2):
            first = half * 128 + which_child * 64
            merge_table[first : first + 64, half * 64 : half * 64 + 64] = block_table.T
    return merge_table


def split_matrices():
    parts = []
    for dimension in range(2):
        exact = merge_matrix(dimension).astype(np.float32)
        high = exact.astype(jnp.bfloat16)
        low = (exact - high.astype(np.float32)).astype(jnp.bfloat16)
        parts += [high, low]
    return np.stack(parts)


def lane_nodes():
    lanes = np.arange(128) % 64
    nodes = chebyshev_nodes()
    return np.stack([nodes[lanes // 8], nodes[lanes % 8]] + [np.zeros(128)] * 6).astype(np.float32)


def level_plan(local_bits, inner_bits, outer_bits):
    levels_total = inner_bits + outer_bits
    carried = [local_bits + level for level in range(levels_total)]
    moved = [
        local_bits - inner_bits + level
        if level < inner_bits
        else local_bits - levels_total + level - inner_bits
        for level in range(levels_total)
    ]
    source = [[], []]
    for level in range(levels_total):
        source[(level + 1) % 2].append(("carried", level))
    source[0] += [local_bits - 7, local_bits - 6, local_bits - 5]
    source[1] += [local_bits - 4, local_bits - 3, local_bits - 2, local_bits - 1]
    target = [[], []]
    for ordinal in range(local_bits - 7):
        target[ordinal % 2].append(ordinal)

    def place(bit):
        if isinstance(bit, tuple):
            return moved[bit[1]]
        if bit in moved:
            return (moved.index(bit),)
        return bit

    source = [[place(bit) for bit in group] for group in source]
    target = [[place(bit) for bit in group] for group in target]
    plan = []
    for level in range(levels_total):
        dimension = (level + 1) % 2
        plan.append(
            (dimension, moved[level], [list(g) for g in target], [list(g) for g in source])
        )
        source[dimension] = source[dimension][1:]
        target[dimension] = [moved[level]] + target[dimension]
    plan.append((None, None, [list(g) for g in target], [list(g) for g in source]))
    return plan


def box_span(source):
    return GRID_N * 2.0 ** (len(source) - TREE_LEVELS)


def sincos(turns):
    near = turns - jnp.floor(turns + 0.5)
    square = near * near
    root = np.sqrt(2.0)
    sine = SINE[3] * root
    for coefficient in SINE[2::-1]:
        sine = sine * square + coefficient * root
    sine = sine * near
    cosine = COSINE[4] * root
    for coefficient in COSINE[3::-1]:
        cosine = cosine * square + coefficient * root
    return sine * cosine, 1.0 - sine * sine


def fit(function, powers):
    grid = 0.25 * (1.0 - np.cos(np.pi * (np.arange(4000) + 0.5) / 4000))
    matrix = np.stack([grid**power for power in powers], 1)
    return [float(v) for v in np.linalg.lstsq(matrix, function(np.pi * grid), rcond=None)[0]]


SINE = fit(np.sin, (1, 3, 5, 7))
COSINE = fit(np.cos, (0, 2, 4, 6, 8))


def combos(bits):
    result = [{}]
    for bit in bits:
        result = [{**one, bit: value} for one in result for value in range(2)]
    return result


def pick(assignment, bits):
    return tuple(assignment[bit] for bit in bits)


def kernel(plan, row_bits, axes, x_ref, matrix_ref, node_ref, out_ref, high_ref, low_ref):
    inner_size = lax.axis_size(axes[1])
    device = lax.axis_index(axes[0]) * inner_size + lax.axis_index(axes[1])
    leading = list(range(row_bits - 1, LOW_BITS - 1, -1))
    rows = lax.broadcasted_iota(jnp.int32, (BLOCK, 128), 0)
    lanes = lax.broadcasted_iota(jnp.int32, (BLOCK, 128), 1)
    low_half = lanes < 64
    child = jnp.where(low_half, 0.0, 1.0)
    row_bit = [(rows >> bit & 1).astype(jnp.float32) for bit in range(LOW_BITS)]
    node = [jnp.broadcast_to(node_ref[d : d + 1, :], (BLOCK, 128)) for d in range(2)]
    device_bit = {}

    def index_tile(places, start):
        total = start
        scalar = None
        for ordinal, where in enumerate(places):
            weight = float(1 << ordinal)
            if isinstance(where, tuple):
                if where[0] not in device_bit:
                    device_bit[where[0]] = (device >> where[0] & 1).astype(jnp.float32)
                term = device_bit[where[0]] * weight
                scalar = term if scalar is None else scalar + term
            elif where < LOW_BITS:
                total = total + row_bit[where] * weight
        return total if scalar is None else total + scalar

    def index_lead(places, assignment):
        return sum(
            float(1 << ordinal) * assignment[where]
            for ordinal, where in enumerate(places)
            if not isinstance(where, tuple) and where in assignment
        )

    def lead_bits(places, free):
        return [w for w in places if not isinstance(w, tuple) and w in free]

    def coefficients(source, free, lane_child):
        trig = []
        bits = [lead_bits(source[d], free) for d in range(2)]
        for d in range(2):
            width = 2.0 ** (-len(source[d]))
            start = node[d] + 0.5
            if lane_child == d:
                start = start + child
            tile = index_tile(source[d], start) * width
            trig.append(
                {
                    pick(one, bits[d]): sincos(tile + index_lead(source[d], one) * width)
                    for one in combos(bits[d])
                }
            )
        table = {}
        for one in combos(bits[0]):
            for two in combos(bits[1]):
                sine_one, cosine_one = trig[0][pick(one, bits[0])]
                sine_two, cosine_two = trig[1][pick(two, bits[1])]
                first = 0.125 + sine_one * sine_two * 0.0625
                second = 0.125 + cosine_one * cosine_two * 0.0625
                table[pick(one, bits[0]), pick(two, bits[1])] = (first * first, second * second)
        return table, bits

    def frequencies(target, source, free):
        result = []
        for d in range(2):
            bits = lead_bits(target[d], free)
            width = box_span(source[d])
            tile = index_tile(target[d], 0.5 * jnp.ones((BLOCK, 128), jnp.float32)) * width
            result.append(
                (
                    bits,
                    {
                        pick(one, bits): tile + (index_lead(target[d], one) * width - GRID_N / 2.0)
                        for one in combos(bits)
                    },
                )
            )
        return result

    def root(value):
        return value * lax.rsqrt(value)

    def pack(first, second):
        return (
            jnp.where(low_half, first, pltpu.roll(second, 64, 1)),
            jnp.where(low_half, pltpu.roll(first, 64, 1), second),
        )

    first_moved = plan[0][1]
    state = {}
    for one in combos([bit for bit in leading if bit != first_moved]):
        halves = []
        for value in range(2):
            full = {**one, first_moved: value}
            start = sum(full[bit] << bit for bit in leading)
            halves.append(x_ref[start : start + BLOCK, :])
        state[pick(one, [b for b in leading if b != first_moved])] = pack(*halves)

    for level, (dimension, moved, target, source) in enumerate(plan[:-1]):
        last = level == len(plan) - 2
        free = [bit for bit in leading if bit != moved]
        if last:
            next_moved = free[0]
        else:
            next_moved = plan[level + 1][1]
        next_free = [bit for bit in leading if bit != next_moved]
        table, source_lead = coefficients(source, free, dimension)
        parents = frequencies(target, source, free)
        quarter = 0.25 * box_span(source[dimension])
        children = [
            {key: value + shift for key, value in parents[dimension][1].items()}
            for shift in (-quarter, quarter)
        ]
        other = 1 - dimension
        slots = {}
        for position, one in enumerate(combos(next_free)):
            slots[pick(one, next_free)] = position
        half_rows = len(slots) * BLOCK
        for one in combos(free):
            real, imaginary = state[pick(one, free)]
            squares = table[pick(one, source_lead[0]), pick(one, source_lead[1])]
            key = [pick(one, parents[d][0]) for d in range(2)]
            k_other = parents[other][1][key[other]]
            k_parent = parents[dimension][1][key[dimension]]
            fixed = squares[other] * (k_other * k_other)
            if level > 0:
                radius = root(fixed + squares[dimension] * (k_parent * k_parent))
            for branch in range(2):
                k_child = children[branch][key[dimension]]
                turns = root(fixed + squares[dimension] * (k_child * k_child))
                if level > 0:
                    scale = 2.0 ** (-len(source[dimension])) * (-quarter, quarter)[branch]
                    turns = (turns - radius) + node[dimension] * scale
                else:
                    turns = turns - jnp.floor(turns)
                    width = [2.0 ** (-len(source[d])) for d in range(2)]
                    turns = turns + (
                        node[dimension] * width[dimension] * k_child
                        + node[other] * width[other] * k_other
                    )
                sine, cosine = sincos(turns)
                full = {**one, moved: branch}
                column = full[next_moved] * 128
                slot = slots[pick(full, next_free)] * BLOCK
                for component, value in enumerate(
                    (real * cosine - imaginary * sine, real * sine + imaginary * cosine)
                ):
                    top = value.astype(jnp.bfloat16)
                    rest = (value - top.astype(jnp.float32)).astype(jnp.bfloat16)
                    place = pl.ds(component * half_rows + slot, BLOCK)
                    high_ref[place, column : column + 128] = top
                    low_ref[place, column : column + 128] = rest
        top, rest = matrix_ref[2 * dimension], matrix_ref[2 * dimension + 1]

        def product(a, b):
            return jnp.dot(a, b, preferred_element_type=jnp.float32)

        merged = product(high_ref[...], top) + product(low_ref[...], top) + product(high_ref[...], rest)
        state = {
            key: (
                merged[slot * BLOCK : (slot + 1) * BLOCK],
                merged[half_rows + slot * BLOCK : half_rows + (slot + 1) * BLOCK],
            )
            for key, slot in slots.items()
        }

    _, _, target, source = plan[-1]
    packed = next_moved
    free = [bit for bit in leading if bit != packed]
    lane_part = [[], []]
    for d in range(2):
        for name, places in (("a", target[d]), ("b", source[d])):
            for ordinal, where in enumerate(places):
                if where == packed:
                    lane_part[d].append((name, float(1 << ordinal)))
    trig, bits = [], [lead_bits(source[d], free) for d in range(2)]
    for d in range(2):
        width = 2.0 ** (-len(source[d]))
        start = node[d] + 0.5
        for name, weight in lane_part[d]:
            if name == "b":
                start = start + child * weight
        tile = index_tile(source[d], start) * width
        trig.append(
            {pick(one, bits[d]): sincos(tile + index_lead(source[d], one) * width) for one in combos(bits[d])}
        )
    centers = frequencies(target, source, free)
    for d in range(2):
        for name, weight in lane_part[d]:
            if name == "a":
                step = child * (weight * box_span(source[d]))
                centers[d] = (centers[d][0], {k: v + step for k, v in centers[d][1].items()})
    for one in combos(free):
        sine_one, cosine_one = trig[0][pick(one, bits[0])]
        sine_two, cosine_two = trig[1][pick(one, bits[1])]
        first = 0.125 + sine_one * sine_two * 0.0625
        second = 0.125 + cosine_one * cosine_two * 0.0625
        k = [centers[d][1][pick(one, centers[d][0])] for d in range(2)]
        first, second = first * k[0], second * k[1]
        turns = root(first * first + second * second)
        turns = turns - jnp.floor(turns)
        width = [2.0 ** (-len(source[d])) for d in range(2)]
        turns = turns + (node[0] * width[0] * k[0] + node[1] * width[1] * k[1])
        sine, cosine = sincos(turns)
        real, imaginary = state[pick(one, free)]
        outputs = pack(real * cosine + imaginary * sine, imaginary * cosine - real * sine)
        for value in range(2):
            full = {**one, packed: value}
            start = sum(full[bit] << bit for bit in leading)
            out_ref[start : start + BLOCK, :] = outputs[value]


def run_levels(rows, plan):
    row_bits = rows.shape[0].bit_length() - 1
    half = rows.shape[0]
    vmem = pl.BlockSpec(memory_space=pltpu.VMEM)
    return pl.pallas_call(
        functools.partial(kernel, plan, row_bits, ("outer", "inner")),
        out_shape=jax.ShapeDtypeStruct(rows.shape, jnp.float32),
        in_specs=[vmem] * 3,
        out_specs=vmem,
        scratch_shapes=[pltpu.VMEM((half, 256), jnp.bfloat16)] * 2,
        compiler_params=pltpu.CompilerParams(vmem_limit_bytes=32 * 1024 * 1024),
    )(rows, jnp.asarray(split_matrices()), jnp.asarray(lane_nodes()))


def reorder_plan(plan, order):
    def place(bit):
        return bit if bit is None or isinstance(bit, tuple) else order.index(bit)

    return [
        (dimension, place(moved), [[place(b) for b in g] for g in target], [[place(b) for b in g] for g in source])
        for dimension, moved, target, source in plan
    ]


def reorder_rows(rows, order):
    count = len(order)
    if list(order) == list(range(count)):
        return rows
    axes = [count - 1 - order[count - 1 - i] for i in range(count)]
    return rows.reshape((2,) * count + (128,)).transpose(axes + [count]).reshape(rows.shape)


def body(weights):
    row_bits = weights.shape[0].bit_length() - 1
    inner_bits = lax.axis_size("inner").bit_length() - 1
    outer_bits = lax.axis_size("outer").bit_length() - 1
    plan = level_plan(row_bits, inner_bits, outer_bits)
    moved = [entry[1] for entry in plan[:-1]]
    rows = lax.all_to_all(weights, ("inner", "outer"), 0, 0, tiled=True)
    level = 0
    while level < len(moved):
        count = 1
        while level + count < len(moved) and count < row_bits - LOW_BITS:
            count += 1
        group = moved[level : level + count]
        order = [bit for bit in range(row_bits) if bit not in group] + sorted(group)
        rows = reorder_rows(rows, order)
        rows = run_levels(rows, reorder_plan(plan[level : level + count + 1], order))
        back = [order.index(bit) for bit in range(row_bits)]
        rows = reorder_rows(rows, back)
        level += count
    return rows


def solution(mesh):
    spec = P(("outer", "inner"), None)
    return jax.shard_map(body, mesh=mesh, in_specs=(spec,), out_specs=spec, check_vma=False)
```

```python
import functools

import jax
import jax.numpy as jnp
import numpy as np
from jax import lax
from jax.experimental import pallas as pl
from jax.experimental.pallas import tpu as pltpu
from jax.sharding import PartitionSpec as P

GRID_N = 16384
TREE_LEVELS = 11
LOW_BITS = 4
BLOCK = 1 << LOW_BITS


def chebyshev_nodes():
    return 0.5 * np.cos(np.pi * (2.0 * np.arange(8) + 1.0) / 16.0)


def lagrange_weights(which_child):
    node_values = chebyshev_nodes()
    targets = (node_values + which_child - 0.5) / 2.0
    weights_table = np.ones((8, 8))
    for anchor in range(8):
        for other_node in range(8):
            if other_node != anchor:
                weights_table[anchor, :] = (
                    weights_table[anchor, :]
                    * (targets - node_values[other_node])
                    / (node_values[anchor] - node_values[other_node])
                )
    return weights_table


def merge_matrix(dimension):
    merge_table = np.zeros((256, 128))
    for which_child in range(2):
        weights_table = lagrange_weights(which_child)
        if dimension == 0:
            block_table = np.kron(weights_table, np.eye(8))
        else:
            block_table = np.kron(np.eye(8), weights_table)
        for half in range(2):
            first = half * 128 + which_child * 64
            merge_table[first : first + 64, half * 64 : half * 64 + 64] = block_table.T
    return merge_table


def split_matrices():
    parts = []
    for dimension in range(2):
        exact = merge_matrix(dimension).astype(np.float32)
        high = exact.astype(jnp.bfloat16)
        low = (exact - high.astype(np.float32)).astype(jnp.bfloat16)
        parts.append(np.concatenate([high, low], 1))
    return np.stack(parts)


def lane_nodes():
    lanes = np.arange(128) % 64
    nodes = chebyshev_nodes()
    return np.stack([nodes[lanes // 8], nodes[lanes % 8]] + [np.zeros(128)] * 6).astype(np.float32)


def level_plan(local_bits, inner_bits, outer_bits):
    levels_total = inner_bits + outer_bits
    carried = [local_bits + level for level in range(levels_total)]
    moved = [
        local_bits - inner_bits + level
        if level < inner_bits
        else local_bits - levels_total + level - inner_bits
        for level in range(levels_total)
    ]
    source = [[], []]
    for level in range(levels_total):
        source[(level + 1) % 2].append(("carried", level))
    source[0] += [local_bits - 7, local_bits - 6, local_bits - 5]
    source[1] += [local_bits - 4, local_bits - 3, local_bits - 2, local_bits - 1]
    target = [[], []]
    for ordinal in range(local_bits - 7):
        target[ordinal % 2].append(ordinal)

    def place(bit):
        if isinstance(bit, tuple):
            return moved[bit[1]]
        if bit in moved:
            return (moved.index(bit),)
        return bit

    source = [[place(bit) for bit in group] for group in source]
    target = [[place(bit) for bit in group] for group in target]
    plan = []
    for level in range(levels_total):
        dimension = (level + 1) % 2
        plan.append(
            (dimension, moved[level], [list(g) for g in target], [list(g) for g in source])
        )
        source[dimension] = source[dimension][1:]
        target[dimension] = [moved[level]] + target[dimension]
    plan.append((None, None, [list(g) for g in target], [list(g) for g in source]))
    return plan


def box_span(source):
    return GRID_N * 2.0 ** (len(source) - TREE_LEVELS)


def reduced(turns):
    return turns - jnp.floor(turns + 0.5)


def odd_series(coefficients, near, square):
    total = coefficients[-1]
    for coefficient in coefficients[-2::-1]:
        total = total * square + coefficient
    return total * near


def sincos(turns):
    near = reduced(turns)
    square = near * near
    sine = odd_series(SINE, near, square)
    cosine = odd_series(COSINE, 1.0, square)
    return sine * cosine, 1.0 - sine * sine


def rotation(turns):
    near = reduced(turns)
    sine = odd_series(SHORT_SINE, near, near * near)
    square = sine * sine
    rest = 2.0 - square
    return sine * (rest * lax.rsqrt(rest)), 1.0 - square


def fit(function, powers):
    grid = 0.25 * (1.0 - np.cos(np.pi * (np.arange(2000) + 0.5) / 2000))
    matrix = np.stack([grid**power for power in powers], 1)
    exact = np.sqrt(2.0) * function(np.pi * grid)
    weight = np.ones_like(grid)
    best = None
    for _ in range(100):
        scale = np.sqrt(weight)
        solved = np.linalg.lstsq(matrix * scale[:, None], exact * scale, rcond=None)[0]
        error = np.abs(matrix @ solved - exact)
        if best is None or error.max() < best[0]:
            best = (error.max(), solved)
        weight = weight * error
        weight = weight / weight.sum()
    return best[1], best[0]


SINE = [float(v) for v in fit(np.sin, (1, 3, 5, 7, 9))[0]]
COSINE = [float(v) for v in fit(np.cos, (0, 2, 4, 6, 8))[0]]
SHORT_SINE, SHORT_ERROR = fit(np.sin, (1, 3, 5, 7))
SHORT_SINE = [float(v) for v in SHORT_SINE * (1.0 - SHORT_ERROR - 6e-7)]


def combos(bits):
    result = [{}]
    for bit in bits:
        result = [{**one, bit: value} for one in result for value in range(2)]
    return result


def pick(assignment, bits):
    return tuple(assignment[bit] for bit in bits)


def kernel(plan, row_bits, axes, x_ref, matrix_ref, node_ref, out_ref):
    inner_size = lax.axis_size(axes[1])
    device = lax.axis_index(axes[0]) * inner_size + lax.axis_index(axes[1])
    leading = list(range(row_bits - 1, LOW_BITS - 1, -1))
    rows = lax.broadcasted_iota(jnp.int32, (BLOCK, 128), 0)
    lanes = lax.broadcasted_iota(jnp.int32, (BLOCK, 128), 1)
    low_half = lanes < 64
    child = jnp.where(low_half, 0.0, 1.0)
    row_bit = [(rows >> bit & 1).astype(jnp.float32) for bit in range(LOW_BITS)]
    node = [jnp.broadcast_to(node_ref[d : d + 1, :], (BLOCK, 128)) for d in range(2)]
    device_bit = {}

    def index_tile(places, start):
        total = start
        scalar = None
        for ordinal, where in enumerate(places):
            weight = float(1 << ordinal)
            if isinstance(where, tuple):
                if where[0] not in device_bit:
                    device_bit[where[0]] = (device >> where[0] & 1).astype(jnp.float32)
                term = device_bit[where[0]] * weight
                scalar = term if scalar is None else scalar + term
            elif where < LOW_BITS:
                total = total + row_bit[where] * weight
        return total if scalar is None else total + scalar

    def index_lead(places, assignment):
        return sum(
            float(1 << ordinal) * assignment[where]
            for ordinal, where in enumerate(places)
            if not isinstance(where, tuple) and where in assignment
        )

    def lead_bits(places, free):
        return [w for w in places if not isinstance(w, tuple) and w in free]

    def coefficients(source, free, lane_child):
        trig = []
        bits = [lead_bits(source[d], free) for d in range(2)]
        for d in range(2):
            width = 2.0 ** (-len(source[d]))
            start = node[d] + 0.5
            if lane_child == d:
                start = start + child
            tile = index_tile(source[d], start) * width
            trig.append(
                {
                    pick(one, bits[d]): sincos(tile + index_lead(source[d], one) * width)
                    for one in combos(bits[d])
                }
            )
        table = {}
        for one in combos(bits[0]):
            for two in combos(bits[1]):
                sine_one, cosine_one = trig[0][pick(one, bits[0])]
                sine_two, cosine_two = trig[1][pick(two, bits[1])]
                first = 0.125 + sine_one * sine_two * 0.0625
                second = 0.125 + cosine_one * cosine_two * 0.0625
                table[pick(one, bits[0]), pick(two, bits[1])] = (first * first, second * second)
        return table, bits

    def frequencies(target, source, free):
        result = []
        for d in range(2):
            bits = lead_bits(target[d], free)
            width = box_span(source[d])
            tile = index_tile(target[d], 0.5 * jnp.ones((BLOCK, 128), jnp.float32)) * width
            result.append(
                (
                    bits,
                    {
                        pick(one, bits): tile + (index_lead(target[d], one) * width - GRID_N / 2.0)
                        for one in combos(bits)
                    },
                )
            )
        return result

    def root(value):
        return value * lax.rsqrt(value)

    def pack(first, second):
        return (
            jnp.where(low_half, first, pltpu.roll(second, 64, 1)),
            jnp.where(low_half, pltpu.roll(first, 64, 1), second),
        )

    first_moved = plan[0][1]
    state = {}
    for one in combos([bit for bit in leading if bit != first_moved]):
        halves = []
        for value in range(2):
            full = {**one, first_moved: value}
            start = sum(full[bit] << bit for bit in leading)
            halves.append(x_ref[start : start + BLOCK, :])
        state[pick(one, [b for b in leading if b != first_moved])] = pack(*halves)

    for level, (dimension, moved, target, source) in enumerate(plan[:-1]):
        last = level == len(plan) - 2
        free = [bit for bit in leading if bit != moved]
        if last:
            next_moved = free[0]
        else:
            next_moved = plan[level + 1][1]
        next_free = [bit for bit in leading if bit != next_moved]
        table, source_lead = coefficients(source, free, dimension)
        parents = frequencies(target, source, free)
        quarter = 0.25 * box_span(source[dimension])
        children = [
            {key: value + shift for key, value in parents[dimension][1].items()}
            for shift in (-quarter, quarter)
        ]
        other = 1 - dimension
        def rotated(one):
            results = []
            real, imaginary = state[pick(one, free)]
            squares = table[pick(one, source_lead[0]), pick(one, source_lead[1])]
            key = [pick(one, parents[d][0]) for d in range(2)]
            k_other = parents[other][1][key[other]]
            k_parent = parents[dimension][1][key[dimension]]
            fixed = squares[other] * (k_other * k_other)
            if level > 0:
                radius = root(fixed + squares[dimension] * (k_parent * k_parent))
                step = node[dimension] * (2.0 ** (-len(source[dimension])) * quarter)
                offsets = (radius + step, radius - step)
            for branch in range(2):
                k_child = children[branch][key[dimension]]
                turns = root(fixed + squares[dimension] * (k_child * k_child))
                if level > 0:
                    turns = turns - offsets[branch]
                else:
                    turns = turns - jnp.floor(turns)
                    width = [2.0 ** (-len(source[d])) for d in range(2)]
                    turns = turns + (
                        node[dimension] * width[dimension] * k_child
                        + node[other] * width[other] * k_other
                    )
                sine, cosine = rotation(turns)
                results.append((real * cosine - imaginary * sine, real * sine + imaginary * cosine))
            return results

        later = {bit: place for place, (_, bit, _, _) in enumerate(plan[:-1])}
        order = sorted(
            (bit for bit in next_free if bit != moved),
            key=lambda bit: -later.get(bit, len(plan)) if later.get(bit, len(plan)) > level else 0,
        )
        matrix = matrix_ref[dimension]
        next_state = {}
        for group in combos(order):
            terms = {}
            for half in range(2):
                one = {**group, next_moved: half}
                for branch, values in enumerate(rotated(one)):
                    for component, value in enumerate(values):
                        top = value.astype(jnp.bfloat16)
                        rest = (value - top.astype(jnp.float32)).astype(jnp.bfloat16)
                        terms[branch, component, half] = (top, rest)
            total = None
            for part in range(2):
                stacked = jnp.concatenate(
                    [
                        jnp.concatenate([terms[branch, component, half][part] for half in range(2)], 1)
                        for branch in range(2)
                        for component in range(2)
                    ],
                    0,
                )
                product = jnp.dot(stacked, matrix, preferred_element_type=jnp.float32)
                total = product if total is None else total + product
            total = total[:, :128] + total[:, 128:]
            for branch in range(2):
                first = 2 * branch * BLOCK
                next_state[pick({**group, moved: branch}, next_free)] = (
                    total[first : first + BLOCK],
                    total[first + BLOCK : first + 2 * BLOCK],
                )
        state = next_state

    _, _, target, source = plan[-1]
    packed = next_moved
    free = [bit for bit in leading if bit != packed]
    lane_part = [[], []]
    for d in range(2):
        for name, places in (("a", target[d]), ("b", source[d])):
            for ordinal, where in enumerate(places):
                if where == packed:
                    lane_part[d].append((name, float(1 << ordinal)))
    trig, bits = [], [lead_bits(source[d], free) for d in range(2)]
    for d in range(2):
        width = 2.0 ** (-len(source[d]))
        start = node[d] + 0.5
        for name, weight in lane_part[d]:
            if name == "b":
                start = start + child * weight
        tile = index_tile(source[d], start) * width
        trig.append(
            {pick(one, bits[d]): sincos(tile + index_lead(source[d], one) * width) for one in combos(bits[d])}
        )
    centers = frequencies(target, source, free)
    for d in range(2):
        for name, weight in lane_part[d]:
            if name == "a":
                step = child * (weight * box_span(source[d]))
                centers[d] = (centers[d][0], {k: v + step for k, v in centers[d][1].items()})
    for one in combos(free):
        sine_one, cosine_one = trig[0][pick(one, bits[0])]
        sine_two, cosine_two = trig[1][pick(one, bits[1])]
        first = 0.125 + sine_one * sine_two * 0.0625
        second = 0.125 + cosine_one * cosine_two * 0.0625
        k = [centers[d][1][pick(one, centers[d][0])] for d in range(2)]
        first, second = first * k[0], second * k[1]
        turns = root(first * first + second * second)
        turns = turns - jnp.floor(turns)
        width = [2.0 ** (-len(source[d])) for d in range(2)]
        turns = turns + (node[0] * width[0] * k[0] + node[1] * width[1] * k[1])
        sine, cosine = rotation(turns)
        real, imaginary = state[pick(one, free)]
        outputs = pack(real * cosine + imaginary * sine, imaginary * cosine - real * sine)
        for value in range(2):
            full = {**one, packed: value}
            start = sum(full[bit] << bit for bit in leading)
            out_ref[start : start + BLOCK, :] = outputs[value]


def run_levels(rows, plan):
    row_bits = rows.shape[0].bit_length() - 1
    vmem = pl.BlockSpec(memory_space=pltpu.VMEM)
    return pl.pallas_call(
        functools.partial(kernel, plan, row_bits, ("outer", "inner")),
        out_shape=jax.ShapeDtypeStruct(rows.shape, jnp.float32),
        in_specs=[vmem] * 3,
        out_specs=vmem,
        compiler_params=pltpu.CompilerParams(vmem_limit_bytes=32 * 1024 * 1024),
    )(rows, jnp.asarray(split_matrices()), jnp.asarray(lane_nodes()))


def reorder_plan(plan, order):
    def place(bit):
        return bit if bit is None or isinstance(bit, tuple) else order.index(bit)

    return [
        (dimension, place(moved), [[place(b) for b in g] for g in target], [[place(b) for b in g] for g in source])
        for dimension, moved, target, source in plan
    ]


def reorder_rows(rows, order):
    count = len(order)
    if list(order) == list(range(count)):
        return rows
    axes = [count - 1 - order[count - 1 - i] for i in range(count)]
    return rows.reshape((2,) * count + (128,)).transpose(axes + [count]).reshape(rows.shape)


def body(weights):
    row_bits = weights.shape[0].bit_length() - 1
    inner_bits = lax.axis_size("inner").bit_length() - 1
    outer_bits = lax.axis_size("outer").bit_length() - 1
    plan = level_plan(row_bits, inner_bits, outer_bits)
    moved = [entry[1] for entry in plan[:-1]]
    rows = lax.all_to_all(weights, ("inner", "outer"), 0, 0, tiled=True)
    level = 0
    while level < len(moved):
        count = 1
        while level + count < len(moved) and count < row_bits - LOW_BITS:
            count += 1
        group = moved[level : level + count]
        order = [bit for bit in range(row_bits) if bit not in group] + sorted(group)
        rows = reorder_rows(rows, order)
        rows = run_levels(rows, reorder_plan(plan[level : level + count + 1], order))
        back = [order.index(bit) for bit in range(row_bits)]
        rows = reorder_rows(rows, back)
        level += count
    return rows


def solution(mesh):
    spec = P(("outer", "inner"), None)
    return jax.shard_map(body, mesh=mesh, in_specs=(spec,), out_specs=spec, check_vma=False)
```

```python
import functools

import jax
import jax.numpy as jnp
import numpy as np
from jax import lax
from jax.experimental import pallas as pl
from jax.experimental.pallas import tpu as pltpu
from jax.sharding import PartitionSpec as P

GRID_N = 16384
TREE_LEVELS = 11
LOW_BITS = 4
BLOCK = 1 << LOW_BITS
VMEM_BYTES = 16 * 1024 * 1024
DOTS = 2


def chebyshev_nodes():
    return 0.5 * np.cos(np.pi * (2.0 * np.arange(8) + 1.0) / 16.0)


def lagrange_weights(which_child):
    node_values = chebyshev_nodes()
    targets = (node_values + which_child - 0.5) / 2.0
    weights_table = np.ones((8, 8))
    for anchor in range(8):
        for other_node in range(8):
            if other_node != anchor:
                weights_table[anchor, :] = (
                    weights_table[anchor, :]
                    * (targets - node_values[other_node])
                    / (node_values[anchor] - node_values[other_node])
                )
    return weights_table


def merge_matrix(dimension):
    merge_table = np.zeros((256, 128))
    for which_child in range(2):
        weights_table = lagrange_weights(which_child)
        if dimension == 0:
            block_table = np.kron(weights_table, np.eye(8))
        else:
            block_table = np.kron(np.eye(8), weights_table)
        for half in range(2):
            first = half * 128 + which_child * 64
            merge_table[first : first + 64, half * 64 : half * 64 + 64] = block_table.T
    return merge_table


def split_matrices():
    parts = []
    for dimension in range(2):
        exact = merge_matrix(dimension).astype(np.float32)
        high = exact.astype(jnp.bfloat16)
        low = (exact - high.astype(np.float32)).astype(jnp.bfloat16)
        parts.append(np.concatenate([high, low], 1))
    return np.stack(parts)


def lane_nodes():
    lanes = np.arange(128) % 64
    nodes = chebyshev_nodes()
    return np.stack([nodes[lanes // 8], nodes[lanes % 8]] + [np.zeros(128)] * 6).astype(np.float32)


def level_plan(local_bits, inner_bits, outer_bits):
    levels_total = inner_bits + outer_bits
    carried = [local_bits + level for level in range(levels_total)]
    moved = [
        local_bits - inner_bits + level
        if level < inner_bits
        else local_bits - levels_total + level - inner_bits
        for level in range(levels_total)
    ]
    source = [[], []]
    for level in range(levels_total):
        source[(level + 1) % 2].append(("carried", level))
    source[0] += [local_bits - 7, local_bits - 6, local_bits - 5]
    source[1] += [local_bits - 4, local_bits - 3, local_bits - 2, local_bits - 1]
    target = [[], []]
    for ordinal in range(local_bits - 7):
        target[ordinal % 2].append(ordinal)

    def place(bit):
        if isinstance(bit, tuple):
            return moved[bit[1]]
        if bit in moved:
            return (moved.index(bit),)
        return bit

    source = [[place(bit) for bit in group] for group in source]
    target = [[place(bit) for bit in group] for group in target]
    plan = []
    for level in range(levels_total):
        dimension = (level + 1) % 2
        plan.append(
            (dimension, moved[level], [list(g) for g in target], [list(g) for g in source])
        )
        source[dimension] = source[dimension][1:]
        target[dimension] = [moved[level]] + target[dimension]
    plan.append((None, None, [list(g) for g in target], [list(g) for g in source]))
    return plan


def box_span(source):
    return GRID_N * 2.0 ** (len(source) - TREE_LEVELS)


def reduced(turns):
    return turns - jnp.floor(turns + 0.5)


def odd_series(coefficients, near, square):
    total = coefficients[-1]
    for coefficient in coefficients[-2::-1]:
        total = total * square + coefficient
    return total * near


def sincos(turns):
    near = turns - lax.round(turns, lax.RoundingMethod.TO_NEAREST_EVEN)
    square = near * near
    sine = series(SINE, square) * near
    cosine = series(COSINE, square)
    return sine * cosine, 1.0 - sine * sine


def series(coefficients, square):
    total = coefficients[-1]
    for coefficient in coefficients[-2::-1]:
        total = total * square + coefficient
    return total


def fit(function, powers):
    grid = 0.25 * (1.0 - np.cos(np.pi * (np.arange(2000) + 0.5) / 2000))
    matrix = np.stack([grid**power for power in powers], 1)
    exact = np.sqrt(2.0) * function(np.pi * grid)
    weight = np.ones_like(grid)
    best = None
    for _ in range(100):
        scale = np.sqrt(weight)
        solved = np.linalg.lstsq(matrix * scale[:, None], exact * scale, rcond=None)[0]
        error = np.abs(matrix @ solved - exact)
        if best is None or error.max() < best[0]:
            best = (error.max(), solved)
        weight = weight * error
        weight = weight / weight.sum()
    return [float(v) for v in best[1]]


SINE = fit(np.sin, (1, 3, 5, 7, 9))
COSINE = fit(np.cos, (0, 2, 4, 6, 8))


def combos(bits):
    result = [{}]
    for bit in bits:
        result = [{**one, bit: value} for one in result for value in range(2)]
    return result


def pick(assignment, bits):
    return tuple(assignment[bit] for bit in bits)


class Layout:
    def __init__(self, plan, row_bits):
        self.plan = plan
        self.leading = list(range(row_bits - 1, LOW_BITS - 1, -1))
        self.moved = [entry[1] for entry in plan[:-1]]
        self.packed = self.moved + [[bit for bit in self.leading if bit != self.moved[-1]][0]]
        self.entries = {}
        for level, packed in enumerate(self.packed):
            free = self.free(level)
            for one in combos(free):
                for branch in range(2 if level < len(self.moved) else 1):
                    self.entries[level, pick(one, free), branch] = len(self.entries)

    def free(self, level):
        return [bit for bit in self.leading if bit != self.packed[level]]

    def place(self, level, one, branch=0):
        first = self.entries[level, pick(one, self.free(level)), branch] * 2 * BLOCK
        return slice(first, first + BLOCK), slice(first + BLOCK, first + 2 * BLOCK)

    def row(self, assignment):
        return sum(assignment[bit] << bit for bit in self.leading if bit in assignment)


def table_kernel(layout, axes, node_ref, table_ref):
    plan = layout.plan
    device = lax.axis_index(axes[0]) * lax.axis_size(axes[1]) + lax.axis_index(axes[1])
    rows = lax.broadcasted_iota(jnp.int32, (BLOCK, 128), 0)
    lanes = lax.broadcasted_iota(jnp.int32, (BLOCK, 128), 1)
    half = jnp.where(lanes < 64, 0.0, 1.0)
    row_bit = [(rows >> bit & 1).astype(jnp.float32) for bit in range(LOW_BITS)]
    node = [jnp.broadcast_to(node_ref[d : d + 1, :], (BLOCK, 128)) for d in range(2)]

    def index_tile(places, packed):
        total = jnp.full((BLOCK, 128), 0.5, jnp.float32)
        scalar = None
        for ordinal, where in enumerate(places):
            weight = float(1 << ordinal)
            if isinstance(where, tuple):
                term = (device >> where[0] & 1).astype(jnp.float32) * weight
                scalar = term if scalar is None else scalar + term
            elif where == packed:
                total = total + half * weight
            elif where < LOW_BITS:
                total = total + row_bit[where] * weight
        return total if scalar is None else total + scalar

    def index_lead(places, assignment):
        return sum(
            float(1 << ordinal) * assignment[where]
            for ordinal, where in enumerate(places)
            if not isinstance(where, tuple) and where in assignment
        )

    def by_lead(places, level, function):
        bits = [w for w in places if not isinstance(w, tuple) and w in layout.free(level)]
        tile = index_tile(places, layout.packed[level])
        values = {pick(one, bits): function(tile + index_lead(places, one)) for one in combos(bits)}
        return lambda one: values[pick(one, bits)]

    def root(value):
        return value * lax.rsqrt(value)

    def store(level, one, branch, turns):
        sine, cosine = sincos(turns)
        for place, value in zip(layout.place(level, one, branch), (cosine, sine)):
            table_ref[place, :] = value

    for level, (dimension, _, target, source) in enumerate(plan):
        width = [2.0 ** (-len(source[d])) for d in range(2)]
        span = [box_span(source[d]) for d in range(2)]
        waves = [
            by_lead(source[d], level, lambda box, d=d: sincos((box + node[d]) * width[d]))
            for d in range(2)
        ]
        center = [
            by_lead(target[d], level, lambda box, d=d: box * span[d] - GRID_N / 2.0)
            for d in range(2)
        ]
        for one in combos(layout.free(level)):
            (sine_one, cosine_one), (sine_two, cosine_two) = (waves[d](one) for d in range(2))
            speed = [0.125 + sine_one * sine_two * 0.0625, 0.125 + cosine_one * cosine_two * 0.0625]
            square = [value * value for value in speed]
            k = [center[d](one) for d in range(2)]
            if level == len(plan) - 1:
                radius = root(square[0] * (k[0] * k[0]) + square[1] * (k[1] * k[1]))
                linear = node[0] * width[0] * k[0] + node[1] * width[1] * k[1]
                store(level, one, 0, (radius - jnp.floor(radius)) + linear)
                continue
            other = 1 - dimension
            fixed = square[other] * (k[other] * k[other])
            radius = root(fixed + square[dimension] * (k[dimension] * k[dimension]))
            for branch in range(2):
                shift = (branch - 0.5) * 0.5 * span[dimension]
                child = k[dimension] + shift
                turns = root(fixed + square[dimension] * (child * child))
                if level > 0:
                    turns = (turns - radius) + node[dimension] * (width[dimension] * shift)
                else:
                    linear = node[dimension] * width[dimension] * child
                    linear = linear + node[other] * width[other] * k[other]
                    turns = (turns - jnp.floor(turns)) + linear
                store(level, one, branch, turns)


def level_kernel(layout, x_ref, table_ref, matrix_ref, out_ref, done_ref, sems):
    low_half = lax.broadcasted_iota(jnp.int32, (BLOCK, 128), 1) < 64
    last = len(layout.moved)

    def pack(first, second):
        return (
            jnp.where(low_half, first, pltpu.roll(second, 64, 1)),
            jnp.where(low_half, pltpu.roll(first, 64, 1), second),
        )

    state = {}
    for one in combos(layout.free(0)):
        halves = []
        for value in range(2):
            first = layout.row({**one, layout.packed[0]: value})
            halves.append(x_ref[first : first + BLOCK, :])
        state[pick(one, layout.free(0))] = pack(*halves)

    for level, moved in enumerate(layout.moved):
        free, packed = layout.free(level), layout.packed[level + 1]
        next_free = layout.free(level + 1)
        matrix = matrix_ref[layout.plan[level][0]]
        later = layout.packed[level + 1 :]
        order = sorted(
            (bit for bit in next_free if bit != moved),
            key=lambda bit: -later.index(bit) if bit in later else 0,
        )
        next_state = {}
        groups = combos(order)
        step = max(1, len(groups) // DOTS)
        for start in range(0, len(groups), step):
            parts = ([], [])
            places = []
            for group in groups[start : start + step]:
                halves = []
                for half in range(2):
                    one = {**group, packed: half}
                    real, imaginary = state[pick(one, free)]
                    turned = []
                    for branch in range(2):
                        cosine, sine = (table_ref[place, :] for place in layout.place(level, one, branch))
                        turned += [real * cosine - imaginary * sine, real * sine + imaginary * cosine]
                    halves.append(turned)
                for index in range(4):
                    value = jnp.concatenate([turned[index] for turned in halves], 1)
                    top = value.astype(jnp.bfloat16)
                    parts[0].append(top)
                    parts[1].append((value - top.astype(jnp.float32)).astype(jnp.bfloat16))
                places += [pick({**group, moved: branch}, next_free) for branch in range(2)]
            total = sum(
                jnp.dot(jnp.concatenate(part, 0), matrix, preferred_element_type=jnp.float32)
                for part in parts
            )
            total = total[:, :128] + total[:, 128:]
            for index, place in enumerate(places):
                first = 2 * index * BLOCK
                next_state[place] = (
                    total[first : first + BLOCK],
                    total[first + BLOCK : first + 2 * BLOCK],
                )
        state = next_state

    packed, free = layout.packed[last], layout.free(last)
    copies = []
    for one in combos(free):
        real, imaginary = state[pick(one, free)]
        cosine, sine = (table_ref[place, :] for place in layout.place(last, one))
        outputs = pack(real * cosine + imaginary * sine, imaginary * cosine - real * sine)
        for value in range(2):
            first = layout.row({**one, packed: value})
            done_ref[first : first + BLOCK, :] = outputs[value]
        if all(one[bit] == 1 for bit in free[2:]):
            for value in range(2):
                shared = {bit: one[bit] for bit in free[:2]}
                piece = pl.ds(layout.row({**shared, packed: value}), BLOCK << len(free) - 2)
                copy = pltpu.make_async_copy(done_ref.at[piece], out_ref.at[piece], sems.at[len(copies)])
                copy.start()
                copies.append(copy)
    for copy in copies:
        copy.wait()


def rotations(layout):
    vmem = pl.BlockSpec(memory_space=pltpu.VMEM)
    rows = 2 * BLOCK * len(layout.entries)
    return pl.pallas_call(
        functools.partial(table_kernel, layout, ("outer", "inner")),
        out_shape=jax.ShapeDtypeStruct((rows, 128), jnp.float32),
        in_specs=[vmem],
        out_specs=vmem,
        compiler_params=pltpu.CompilerParams(vmem_limit_bytes=VMEM_BYTES),
        cost_estimate=pl.CostEstimate(
            flops=rows * 128 * 20, bytes_accessed=rows * 512, transcendentals=rows * 128
        ),
    )(jnp.asarray(lane_nodes()))


def run_levels(rows, table, layout):
    vmem = pl.BlockSpec(memory_space=pltpu.VMEM)
    return pl.pallas_call(
        functools.partial(level_kernel, layout),
        out_shape=jax.ShapeDtypeStruct(rows.shape, jnp.float32),
        in_specs=[vmem] * 3,
        out_specs=pl.BlockSpec(memory_space=pl.ANY),
        scratch_shapes=[pltpu.VMEM(rows.shape, jnp.float32), pltpu.SemaphoreType.DMA((8,))],
        compiler_params=pltpu.CompilerParams(vmem_limit_bytes=VMEM_BYTES),
    )(rows, table, jnp.asarray(split_matrices()))


def reorder_plan(plan, order):
    def place(bit):
        return bit if bit is None or isinstance(bit, tuple) else order.index(bit)

    return [
        (dimension, place(moved), [[place(b) for b in g] for g in target], [[place(b) for b in g] for g in source])
        for dimension, moved, target, source in plan
    ]


def reorder_rows(rows, order):
    count = len(order)
    if list(order) == list(range(count)):
        return rows
    axes = [count - 1 - order[count - 1 - i] for i in range(count)]
    return rows.reshape((2,) * count + (128,)).transpose(axes + [count]).reshape(rows.shape)


def level_groups(plan, row_bits):
    moved = [entry[1] for entry in plan[:-1]]
    groups = []
    level = 0
    while level < len(moved):
        count = min(len(moved) - level, row_bits - LOW_BITS)
        group = moved[level : level + count]
        order = [bit for bit in range(row_bits) if bit not in group] + sorted(group)
        groups.append((order, Layout(reorder_plan(plan[level : level + count + 1], order), row_bits)))
        level += count
    return groups


def body(weights):
    row_bits = weights.shape[0].bit_length() - 1
    inner_bits = lax.axis_size("inner").bit_length() - 1
    outer_bits = lax.axis_size("outer").bit_length() - 1
    groups = level_groups(level_plan(row_bits, inner_bits, outer_bits), row_bits)
    rows = lax.all_to_all(weights, ("inner", "outer"), 0, 0, tiled=True)
    tables = [rotations(layout) for _, layout in groups]
    for (order, layout), table in zip(groups, tables):
        rows = run_levels(reorder_rows(rows, order), table, layout)
        rows = reorder_rows(rows, [order.index(bit) for bit in range(row_bits)])
    return rows


def solution(mesh):
    spec = P(("outer", "inner"), None)
    return jax.shard_map(body, mesh=mesh, in_specs=(spec,), out_specs=spec, check_vma=False)
```

```python
import functools

import jax
import jax.numpy as jnp
import numpy as np
from jax import lax
from jax.experimental import pallas as pl
from jax.experimental.pallas import tpu as pltpu
from jax.sharding import PartitionSpec as P

GRID_N = 16384
TREE_LEVELS = 11
LOW_BITS = 4
BLOCK = 1 << LOW_BITS
VMEM_BYTES = 16 * 1024 * 1024
DOTS = 2


def chebyshev_nodes():
    return 0.5 * np.cos(np.pi * (2.0 * np.arange(8) + 1.0) / 16.0)


def lagrange_weights(which_child):
    node_values = chebyshev_nodes()
    targets = (node_values + which_child - 0.5) / 2.0
    weights_table = np.ones((8, 8))
    for anchor in range(8):
        for other_node in range(8):
            if other_node != anchor:
                weights_table[anchor, :] = (
                    weights_table[anchor, :]
                    * (targets - node_values[other_node])
                    / (node_values[anchor] - node_values[other_node])
                )
    return weights_table


def merge_matrix(dimension):
    merge_table = np.zeros((256, 128))
    for which_child in range(2):
        weights_table = lagrange_weights(which_child)
        if dimension == 0:
            block_table = np.kron(weights_table, np.eye(8))
        else:
            block_table = np.kron(np.eye(8), weights_table)
        for half in range(2):
            first = half * 128 + which_child * 64
            merge_table[first : first + 64, half * 64 : half * 64 + 64] = block_table.T
    return merge_table


def split_matrices():
    parts = []
    for dimension in range(2):
        exact = merge_matrix(dimension).astype(np.float32)
        high = exact.astype(jnp.bfloat16)
        low = (exact - high.astype(np.float32)).astype(jnp.bfloat16)
        parts.append(np.concatenate([high, low], 1))
    return np.stack(parts)


def lane_nodes():
    lanes = np.arange(128) % 64
    nodes = chebyshev_nodes()
    return np.stack([nodes[lanes // 8], nodes[lanes % 8]] + [np.zeros(128)] * 6).astype(np.float32)


def level_plan(local_bits, inner_bits, outer_bits):
    levels_total = inner_bits + outer_bits
    carried = [local_bits + level for level in range(levels_total)]
    moved = [
        local_bits - inner_bits + level
        if level < inner_bits
        else local_bits - levels_total + level - inner_bits
        for level in range(levels_total)
    ]
    source = [[], []]
    for level in range(levels_total):
        source[(level + 1) % 2].append(("carried", level))
    source[0] += [local_bits - 7, local_bits - 6, local_bits - 5]
    source[1] += [local_bits - 4, local_bits - 3, local_bits - 2, local_bits - 1]
    target = [[], []]
    for ordinal in range(local_bits - 7):
        target[ordinal % 2].append(ordinal)

    def place(bit):
        if isinstance(bit, tuple):
            return moved[bit[1]]
        if bit in moved:
            return (moved.index(bit),)
        return bit

    source = [[place(bit) for bit in group] for group in source]
    target = [[place(bit) for bit in group] for group in target]
    plan = []
    for level in range(levels_total):
        dimension = (level + 1) % 2
        plan.append(
            (dimension, moved[level], [list(g) for g in target], [list(g) for g in source])
        )
        source[dimension] = source[dimension][1:]
        target[dimension] = [moved[level]] + target[dimension]
    plan.append((None, None, [list(g) for g in target], [list(g) for g in source]))
    return plan


def box_span(source):
    return GRID_N * 2.0 ** (len(source) - TREE_LEVELS)


def reduced(turns):
    return turns - jnp.floor(turns + 0.5)


def odd_series(coefficients, near, square):
    total = coefficients[-1]
    for coefficient in coefficients[-2::-1]:
        total = total * square + coefficient
    return total * near


def sincos(turns):
    near = turns - lax.round(turns, lax.RoundingMethod.TO_NEAREST_EVEN)
    square = near * near
    sine = series(SINE, square) * near
    cosine = series(COSINE, square)
    return sine * cosine, 1.0 - sine * sine


def series(coefficients, square):
    total = coefficients[-1]
    for coefficient in coefficients[-2::-1]:
        total = total * square + coefficient
    return total


def fit(function, powers):
    grid = 0.25 * (1.0 - np.cos(np.pi * (np.arange(2000) + 0.5) / 2000))
    matrix = np.stack([grid**power for power in powers], 1)
    exact = np.sqrt(2.0) * function(np.pi * grid)
    weight = np.ones_like(grid)
    best = None
    for _ in range(100):
        scale = np.sqrt(weight)
        solved = np.linalg.lstsq(matrix * scale[:, None], exact * scale, rcond=None)[0]
        error = np.abs(matrix @ solved - exact)
        if best is None or error.max() < best[0]:
            best = (error.max(), solved)
        weight = weight * error
        weight = weight / weight.sum()
    return [float(v) for v in best[1]]


SINE = fit(np.sin, (1, 3, 5, 7, 9))
COSINE = fit(np.cos, (0, 2, 4, 6, 8))


def combos(bits):
    result = [{}]
    for bit in bits:
        result = [{**one, bit: value} for one in result for value in range(2)]
    return result


def pick(assignment, bits):
    return tuple(assignment[bit] for bit in bits)


class Layout:
    def __init__(self, plan, row_bits):
        self.plan = plan
        self.leading = list(range(row_bits - 1, LOW_BITS - 1, -1))
        self.moved = [entry[1] for entry in plan[:-1]]
        self.packed = self.moved + [[bit for bit in self.leading if bit != self.moved[-1]][0]]
        self.entries = {}
        for level, packed in enumerate(self.packed):
            free = self.free(level)
            for one in combos(free):
                for branch in range(2 if level < len(self.moved) else 1):
                    self.entries[level, pick(one, free), branch] = len(self.entries)

    def free(self, level):
        return [bit for bit in self.leading if bit != self.packed[level]]

    def place(self, level, one, branch=0):
        first = self.entries[level, pick(one, self.free(level)), branch] * 2 * BLOCK
        return slice(first, first + BLOCK), slice(first + BLOCK, first + 2 * BLOCK)

    def row(self, assignment):
        return sum(assignment[bit] << bit for bit in self.leading if bit in assignment)


def table_kernel(layout, axes, node_ref, table_ref):
    plan = layout.plan
    device = lax.axis_index(axes[0]) * lax.axis_size(axes[1]) + lax.axis_index(axes[1])
    rows = lax.broadcasted_iota(jnp.int32, (BLOCK, 128), 0)
    lanes = lax.broadcasted_iota(jnp.int32, (BLOCK, 128), 1)
    half = jnp.where(lanes < 64, 0.0, 1.0)
    row_bit = [(rows >> bit & 1).astype(jnp.float32) for bit in range(LOW_BITS)]
    node = [jnp.broadcast_to(node_ref[d : d + 1, :], (BLOCK, 128)) for d in range(2)]

    def index_tile(places, packed):
        total = jnp.full((BLOCK, 128), 0.5, jnp.float32)
        scalar = None
        for ordinal, where in enumerate(places):
            weight = float(1 << ordinal)
            if isinstance(where, tuple):
                term = (device >> where[0] & 1).astype(jnp.float32) * weight
                scalar = term if scalar is None else scalar + term
            elif where == packed:
                total = total + half * weight
            elif where < LOW_BITS:
                total = total + row_bit[where] * weight
        return total if scalar is None else total + scalar

    def index_lead(places, assignment):
        return sum(
            float(1 << ordinal) * assignment[where]
            for ordinal, where in enumerate(places)
            if not isinstance(where, tuple) and where in assignment
        )

    def by_lead(places, level, function):
        bits = [w for w in places if not isinstance(w, tuple) and w in layout.free(level)]
        tile = index_tile(places, layout.packed[level])
        values = {pick(one, bits): function(tile + index_lead(places, one)) for one in combos(bits)}
        return lambda one: values[pick(one, bits)]

    def root(value):
        return value * lax.rsqrt(value)

    def store(level, one, branch, turns):
        sine, cosine = sincos(turns)
        for place, value in zip(layout.place(level, one, branch), (cosine, sine)):
            table_ref[place, :] = value

    for level, (dimension, _, target, source) in enumerate(plan):
        width = [2.0 ** (-len(source[d])) for d in range(2)]
        span = [box_span(source[d]) for d in range(2)]
        waves = [
            by_lead(source[d], level, lambda box, d=d: sincos((box + node[d]) * width[d]))
            for d in range(2)
        ]
        center = [
            by_lead(target[d], level, lambda box, d=d: box * span[d] - GRID_N / 2.0)
            for d in range(2)
        ]
        for one in combos(layout.free(level)):
            (sine_one, cosine_one), (sine_two, cosine_two) = (waves[d](one) for d in range(2))
            speed = [0.125 + sine_one * sine_two * 0.0625, 0.125 + cosine_one * cosine_two * 0.0625]
            square = [value * value for value in speed]
            k = [center[d](one) for d in range(2)]
            if level == len(plan) - 1:
                radius = root(square[0] * (k[0] * k[0]) + square[1] * (k[1] * k[1]))
                linear = node[0] * width[0] * k[0] + node[1] * width[1] * k[1]
                store(level, one, 0, (radius - jnp.floor(radius)) + linear)
                continue
            other = 1 - dimension
            fixed = square[other] * (k[other] * k[other])
            radius = root(fixed + square[dimension] * (k[dimension] * k[dimension]))
            for branch in range(2):
                shift = (branch - 0.5) * 0.5 * span[dimension]
                child = k[dimension] + shift
                turns = root(fixed + square[dimension] * (child * child))
                if level > 0:
                    turns = (turns - radius) + node[dimension] * (width[dimension] * shift)
                else:
                    linear = node[dimension] * width[dimension] * child
                    linear = linear + node[other] * width[other] * k[other]
                    turns = (turns - jnp.floor(turns)) + linear
                store(level, one, branch, turns)


def level_kernel(layout, x_ref, table_ref, matrix_ref, out_ref, done_ref, sems):
    low_half = lax.broadcasted_iota(jnp.int32, (BLOCK, 128), 1) < 64
    last = len(layout.moved)

    def pack(first, second):
        return (
            jnp.where(low_half, first, pltpu.roll(second, 64, 1)),
            jnp.where(low_half, pltpu.roll(first, 64, 1), second),
        )

    state = {}
    for one in combos(layout.free(0)):
        halves = []
        for value in range(2):
            first = layout.row({**one, layout.packed[0]: value})
            halves.append(x_ref[first : first + BLOCK, :])
        state[pick(one, layout.free(0))] = pack(*halves)

    for level, moved in enumerate(layout.moved):
        free, packed = layout.free(level), layout.packed[level + 1]
        next_free = layout.free(level + 1)
        matrix = matrix_ref[layout.plan[level][0]]
        later = layout.packed[level + 1 :]
        order = sorted(
            (bit for bit in next_free if bit != moved),
            key=lambda bit: -later.index(bit) if bit in later else 0,
        )
        next_state = {}
        groups = combos(order)
        step = max(1, len(groups) // DOTS)
        for start in range(0, len(groups), step):
            parts = []
            places = []
            for group in groups[start : start + step]:
                halves = []
                for half in range(2):
                    one = {**group, packed: half}
                    real, imaginary = state[pick(one, free)]
                    turned = []
                    for branch in range(2):
                        cosine, sine = (table_ref[place, :] for place in layout.place(level, one, branch))
                        turned += [real * cosine - imaginary * sine, real * sine + imaginary * cosine]
                    halves.append(turned)
                values = [jnp.concatenate([turned[index] for turned in halves], 1) for index in range(4)]
                tops = [value.astype(jnp.bfloat16) for value in values]
                parts += tops
                parts += [
                    (value - top.astype(jnp.float32)).astype(jnp.bfloat16)
                    for value, top in zip(values, tops)
                ]
                places += [pick({**group, moved: branch}, next_free) for branch in range(2)]
            product = jnp.dot(jnp.concatenate(parts, 0), matrix, preferred_element_type=jnp.float32)
            for index, place in enumerate(places):
                first = (index // 2 * 8 + index % 2 * 2) * BLOCK
                pair = []
                for component in range(2):
                    top = product[first + component * BLOCK : first + (component + 1) * BLOCK]
                    rest = product[first + (component + 4) * BLOCK : first + (component + 5) * BLOCK]
                    pair.append((top[:, 128:] + rest[:, :128]) + top[:, :128])
                next_state[place] = pair
        state = next_state

    packed, free = layout.packed[last], layout.free(last)
    copies = []
    for one in combos(free):
        real, imaginary = state[pick(one, free)]
        cosine, sine = (table_ref[place, :] for place in layout.place(last, one))
        outputs = pack(real * cosine + imaginary * sine, imaginary * cosine - real * sine)
        for value in range(2):
            first = layout.row({**one, packed: value})
            done_ref[first : first + BLOCK, :] = outputs[value]
        if all(one[bit] == 1 for bit in free[2:]):
            for value in range(2):
                shared = {bit: one[bit] for bit in free[:2]}
                piece = pl.ds(layout.row({**shared, packed: value}), BLOCK << len(free) - 2)
                copy = pltpu.make_async_copy(done_ref.at[piece], out_ref.at[piece], sems.at[len(copies)])
                copy.start()
                copies.append(copy)
    for copy in copies:
        copy.wait()


def rotations(layout):
    vmem = pl.BlockSpec(memory_space=pltpu.VMEM)
    rows = 2 * BLOCK * len(layout.entries)
    return pl.pallas_call(
        functools.partial(table_kernel, layout, ("outer", "inner")),
        out_shape=jax.ShapeDtypeStruct((rows, 128), jnp.float32),
        in_specs=[vmem],
        out_specs=vmem,
        compiler_params=pltpu.CompilerParams(vmem_limit_bytes=VMEM_BYTES),
        cost_estimate=pl.CostEstimate(
            flops=rows * 128 * 20, bytes_accessed=rows * 512, transcendentals=rows * 128
        ),
    )(jnp.asarray(lane_nodes()))


def run_levels(rows, table, layout):
    vmem = pl.BlockSpec(memory_space=pltpu.VMEM)
    return pl.pallas_call(
        functools.partial(level_kernel, layout),
        out_shape=jax.ShapeDtypeStruct(rows.shape, jnp.float32),
        in_specs=[vmem] * 3,
        out_specs=pl.BlockSpec(memory_space=pl.ANY),
        scratch_shapes=[pltpu.VMEM(rows.shape, jnp.float32), pltpu.SemaphoreType.DMA((8,))],
        compiler_params=pltpu.CompilerParams(vmem_limit_bytes=VMEM_BYTES),
    )(rows, table, jnp.asarray(split_matrices()))


def reorder_plan(plan, order):
    def place(bit):
        return bit if bit is None or isinstance(bit, tuple) else order.index(bit)

    return [
        (dimension, place(moved), [[place(b) for b in g] for g in target], [[place(b) for b in g] for g in source])
        for dimension, moved, target, source in plan
    ]


def reorder_rows(rows, order):
    count = len(order)
    if list(order) == list(range(count)):
        return rows
    axes = [count - 1 - order[count - 1 - i] for i in range(count)]
    return rows.reshape((2,) * count + (128,)).transpose(axes + [count]).reshape(rows.shape)


def level_groups(plan, row_bits):
    moved = [entry[1] for entry in plan[:-1]]
    groups = []
    level = 0
    while level < len(moved):
        count = min(len(moved) - level, row_bits - LOW_BITS)
        group = moved[level : level + count]
        order = [bit for bit in range(row_bits) if bit not in group] + sorted(group)
        groups.append((order, Layout(reorder_plan(plan[level : level + count + 1], order), row_bits)))
        level += count
    return groups


def body(weights):
    row_bits = weights.shape[0].bit_length() - 1
    inner_bits = lax.axis_size("inner").bit_length() - 1
    outer_bits = lax.axis_size("outer").bit_length() - 1
    groups = level_groups(level_plan(row_bits, inner_bits, outer_bits), row_bits)
    rows = lax.all_to_all(weights, ("inner", "outer"), 0, 0, tiled=True)
    tables = [rotations(layout) for _, layout in groups]
    for (order, layout), table in zip(groups, tables):
        rows = run_levels(reorder_rows(rows, order), table, layout)
        rows = reorder_rows(rows, [order.index(bit) for bit in range(row_bits)])
    return rows


def solution(mesh):
    spec = P(("outer", "inner"), None)
    return jax.shard_map(body, mesh=mesh, in_specs=(spec,), out_specs=spec, check_vma=False)
```

```python
import functools

import jax
import jax.numpy as jnp
import numpy as np
from jax import lax
from jax.experimental import pallas as pl
from jax.experimental.pallas import tpu as pltpu
from jax.sharding import PartitionSpec as P

GRID_N = 16384
TREE_LEVELS = 11
LOW_BITS = 3
BLOCK = 1 << LOW_BITS
VMEM_BYTES = 16 * 1024 * 1024
DOTS = 4


def chebyshev_nodes():
    return 0.5 * np.cos(np.pi * (2.0 * np.arange(8) + 1.0) / 16.0)


def lagrange_weights(which_child):
    node_values = chebyshev_nodes()
    targets = (node_values + which_child - 0.5) / 2.0
    weights_table = np.ones((8, 8))
    for anchor in range(8):
        for other_node in range(8):
            if other_node != anchor:
                weights_table[anchor, :] = (
                    weights_table[anchor, :]
                    * (targets - node_values[other_node])
                    / (node_values[anchor] - node_values[other_node])
                )
    return weights_table


def merge_matrix(dimension):
    merge_table = np.zeros((256, 128))
    for which_child in range(2):
        weights_table = lagrange_weights(which_child)
        if dimension == 0:
            block_table = np.kron(weights_table, np.eye(8))
        else:
            block_table = np.kron(np.eye(8), weights_table)
        for half in range(2):
            first = half * 128 + which_child * 64
            merge_table[first : first + 64, half * 64 : half * 64 + 64] = block_table.T
    return merge_table


def split_matrices():
    parts = []
    for dimension in range(2):
        exact = merge_matrix(dimension).astype(np.float32)
        high = exact.astype(jnp.bfloat16)
        low = (exact - high.astype(np.float32)).astype(jnp.bfloat16)
        parts.append(np.concatenate([high, low], 1))
    return np.stack(parts)


def lane_nodes():
    lanes = np.arange(128) % 64
    nodes = chebyshev_nodes()
    return np.stack([nodes[lanes // 8], nodes[lanes % 8]] + [np.zeros(128)] * 6).astype(np.float32)


def level_plan(local_bits, inner_bits, outer_bits):
    levels_total = inner_bits + outer_bits
    carried = [local_bits + level for level in range(levels_total)]
    moved = [
        local_bits - inner_bits + level
        if level < inner_bits
        else local_bits - levels_total + level - inner_bits
        for level in range(levels_total)
    ]
    source = [[], []]
    for level in range(levels_total):
        source[(level + 1) % 2].append(("carried", level))
    source[0] += [local_bits - 7, local_bits - 6, local_bits - 5]
    source[1] += [local_bits - 4, local_bits - 3, local_bits - 2, local_bits - 1]
    target = [[], []]
    for ordinal in range(local_bits - 7):
        target[ordinal % 2].append(ordinal)

    def place(bit):
        if isinstance(bit, tuple):
            return moved[bit[1]]
        if bit in moved:
            return (moved.index(bit),)
        return bit

    source = [[place(bit) for bit in group] for group in source]
    target = [[place(bit) for bit in group] for group in target]
    plan = []
    for level in range(levels_total):
        dimension = (level + 1) % 2
        plan.append(
            (dimension, moved[level], [list(g) for g in target], [list(g) for g in source])
        )
        source[dimension] = source[dimension][1:]
        target[dimension] = [moved[level]] + target[dimension]
    plan.append((None, None, [list(g) for g in target], [list(g) for g in source]))
    return plan


def box_span(source):
    return GRID_N * 2.0 ** (len(source) - TREE_LEVELS)


def reduced(turns):
    return turns - jnp.floor(turns + 0.5)


def odd_series(coefficients, near, square):
    total = coefficients[-1]
    for coefficient in coefficients[-2::-1]:
        total = total * square + coefficient
    return total * near


def sincos(turns):
    near = turns - lax.round(turns, lax.RoundingMethod.TO_NEAREST_EVEN)
    square = near * near
    sine = series(SINE, square) * near
    cosine = series(COSINE, square)
    return sine * cosine, 1.0 - sine * sine


def series(coefficients, square):
    total = coefficients[-1]
    for coefficient in coefficients[-2::-1]:
        total = total * square + coefficient
    return total


def fit(function, powers):
    grid = 0.25 * (1.0 - np.cos(np.pi * (np.arange(2000) + 0.5) / 2000))
    matrix = np.stack([grid**power for power in powers], 1)
    exact = np.sqrt(2.0) * function(np.pi * grid)
    weight = np.ones_like(grid)
    best = None
    for _ in range(100):
        scale = np.sqrt(weight)
        solved = np.linalg.lstsq(matrix * scale[:, None], exact * scale, rcond=None)[0]
        error = np.abs(matrix @ solved - exact)
        if best is None or error.max() < best[0]:
            best = (error.max(), solved)
        weight = weight * error
        weight = weight / weight.sum()
    return [float(v) for v in best[1]]


SINE = fit(np.sin, (1, 3, 5, 7, 9))
COSINE = fit(np.cos, (0, 2, 4, 6, 8))


def combos(bits):
    result = [{}]
    for bit in bits:
        result = [{**one, bit: value} for one in result for value in range(2)]
    return result


def pick(assignment, bits):
    return tuple(assignment[bit] for bit in bits)


class Layout:
    def __init__(self, plan, row_bits):
        self.plan = plan
        self.leading = list(range(row_bits - 1, LOW_BITS - 1, -1))
        self.moved = [entry[1] for entry in plan[:-1]]
        self.packed = self.moved + [[bit for bit in self.leading if bit != self.moved[-1]][0]]
        self.entries = {}
        for level, packed in enumerate(self.packed):
            free = self.free(level)
            for one in combos(free):
                for branch in range(2 if level < len(self.moved) else 1):
                    self.entries[level, pick(one, free), branch] = len(self.entries)

    def free(self, level):
        return [bit for bit in self.leading if bit != self.packed[level]]

    def place(self, level, one, branch=0):
        first = self.entries[level, pick(one, self.free(level)), branch] * 2 * BLOCK
        return slice(first, first + BLOCK), slice(first + BLOCK, first + 2 * BLOCK)

    def row(self, assignment):
        return sum(assignment[bit] << bit for bit in self.leading if bit in assignment)


def table_kernel(layout, axes, node_ref, table_ref):
    plan = layout.plan
    device = lax.axis_index(axes[0]) * lax.axis_size(axes[1]) + lax.axis_index(axes[1])
    rows = lax.broadcasted_iota(jnp.int32, (BLOCK, 128), 0)
    lanes = lax.broadcasted_iota(jnp.int32, (BLOCK, 128), 1)
    half = jnp.where(lanes < 64, 0.0, 1.0)
    row_bit = [(rows >> bit & 1).astype(jnp.float32) for bit in range(LOW_BITS)]
    node = [jnp.broadcast_to(node_ref[d : d + 1, :], (BLOCK, 128)) for d in range(2)]

    def index_tile(places, packed):
        total = jnp.full((BLOCK, 128), 0.5, jnp.float32)
        scalar = None
        for ordinal, where in enumerate(places):
            weight = float(1 << ordinal)
            if isinstance(where, tuple):
                term = (device >> where[0] & 1).astype(jnp.float32) * weight
                scalar = term if scalar is None else scalar + term
            elif where == packed:
                total = total + half * weight
            elif where < LOW_BITS:
                total = total + row_bit[where] * weight
        return total if scalar is None else total + scalar

    def index_lead(places, assignment):
        return sum(
            float(1 << ordinal) * assignment[where]
            for ordinal, where in enumerate(places)
            if not isinstance(where, tuple) and where in assignment
        )

    def by_lead(places, level, function):
        bits = [w for w in places if not isinstance(w, tuple) and w in layout.free(level)]
        tile = index_tile(places, layout.packed[level])
        values = {pick(one, bits): function(tile + index_lead(places, one)) for one in combos(bits)}
        return lambda one: values[pick(one, bits)]

    def root(value):
        return value * lax.rsqrt(value)

    def store(level, one, branch, turns):
        sine, cosine = sincos(turns)
        for place, value in zip(layout.place(level, one, branch), (cosine, sine)):
            table_ref[place, :] = value

    for level, (dimension, _, target, source) in enumerate(plan):
        width = [2.0 ** (-len(source[d])) for d in range(2)]
        span = [box_span(source[d]) for d in range(2)]
        waves = [
            by_lead(source[d], level, lambda box, d=d: sincos((box + node[d]) * width[d]))
            for d in range(2)
        ]
        center = [
            by_lead(target[d], level, lambda box, d=d: box * span[d] - GRID_N / 2.0)
            for d in range(2)
        ]
        for one in combos(layout.free(level)):
            (sine_one, cosine_one), (sine_two, cosine_two) = (waves[d](one) for d in range(2))
            speed = [0.125 + sine_one * sine_two * 0.0625, 0.125 + cosine_one * cosine_two * 0.0625]
            square = [value * value for value in speed]
            k = [center[d](one) for d in range(2)]
            if level == len(plan) - 1:
                radius = root(square[0] * (k[0] * k[0]) + square[1] * (k[1] * k[1]))
                linear = node[0] * width[0] * k[0] + node[1] * width[1] * k[1]
                store(level, one, 0, (radius - jnp.floor(radius)) + linear)
                continue
            other = 1 - dimension
            fixed = square[other] * (k[other] * k[other])
            radius = root(fixed + square[dimension] * (k[dimension] * k[dimension]))
            for branch in range(2):
                shift = (branch - 0.5) * 0.5 * span[dimension]
                child = k[dimension] + shift
                turns = root(fixed + square[dimension] * (child * child))
                if level > 0:
                    turns = (turns - radius) + node[dimension] * (width[dimension] * shift)
                else:
                    linear = node[dimension] * width[dimension] * child
                    linear = linear + node[other] * width[other] * k[other]
                    turns = (turns - jnp.floor(turns)) + linear
                store(level, one, branch, turns)


def level_kernel(layout, x_ref, table_ref, matrix_ref, out_ref, done_ref, sems):
    low_half = lax.broadcasted_iota(jnp.int32, (BLOCK, 128), 1) < 64
    last = len(layout.moved)

    def pack(first, second):
        return (
            jnp.where(low_half, first, pltpu.roll(second, 64, 1)),
            jnp.where(low_half, pltpu.roll(first, 64, 1), second),
        )

    state = {}
    for one in combos(layout.free(0)):
        halves = []
        for value in range(2):
            first = layout.row({**one, layout.packed[0]: value})
            halves.append(x_ref[first : first + BLOCK, :])
        state[pick(one, layout.free(0))] = pack(*halves)

    for level, moved in enumerate(layout.moved):
        free, packed = layout.free(level), layout.packed[level + 1]
        next_free = layout.free(level + 1)
        matrix = matrix_ref[layout.plan[level][0]]
        later = layout.packed[level + 1 :]
        order = sorted(
            (bit for bit in next_free if bit != moved),
            key=lambda bit: -later.index(bit) if bit in later else -99 * (bit not in layout.packed),
        )
        next_state = {}
        groups = combos(order)
        step = max(1, len(groups) // DOTS)
        for start in range(0, len(groups), step):
            parts = []
            places = []
            for group in groups[start : start + step]:
                halves = []
                for half in range(2):
                    one = {**group, packed: half}
                    real, imaginary = state[pick(one, free)]
                    turned = []
                    for branch in range(2):
                        cosine, sine = (table_ref[place, :] for place in layout.place(level, one, branch))
                        both = (real * cosine - imaginary * sine, real * sine + imaginary * cosine)
                        turned.append(jnp.concatenate(both, 0))
                    halves.append(turned)
                values = [jnp.concatenate([turned[branch] for turned in halves], 1) for branch in range(2)]
                tops = [value.astype(jnp.bfloat16) for value in values]
                parts += tops
                parts += [
                    (value - top.astype(jnp.float32)).astype(jnp.bfloat16)
                    for value, top in zip(values, tops)
                ]
                places += [pick({**group, moved: branch}, next_free) for branch in range(2)]
            product = jnp.dot(jnp.concatenate(parts, 0), matrix, preferred_element_type=jnp.float32)
            for index, place in enumerate(places):
                first = (index // 2 * 4 + index % 2) * 2 * BLOCK
                top = product[first : first + 2 * BLOCK]
                rest = product[first + 4 * BLOCK : first + 6 * BLOCK]
                total = (top[:, 128:] + rest[:, :128]) + top[:, :128]
                next_state[place] = (total[:BLOCK], total[BLOCK:])
        state = next_state

    packed, free = layout.packed[last], layout.free(last)
    copies = []
    for one in combos(free):
        real, imaginary = state[pick(one, free)]
        cosine, sine = (table_ref[place, :] for place in layout.place(last, one))
        outputs = pack(real * cosine + imaginary * sine, imaginary * cosine - real * sine)
        for value in range(2):
            first = layout.row({**one, packed: value})
            done_ref[first : first + BLOCK, :] = outputs[value]
        if all(one[bit] == 1 for bit in free[2:]):
            for value in range(2):
                shared = {bit: one[bit] for bit in free[:2]}
                piece = pl.ds(layout.row({**shared, packed: value}), BLOCK << len(free) - 2)
                copy = pltpu.make_async_copy(done_ref.at[piece], out_ref.at[piece], sems.at[len(copies)])
                copy.start()
                copies.append(copy)
    for copy in copies:
        copy.wait()


def rotations(layout):
    vmem = pl.BlockSpec(memory_space=pltpu.VMEM)
    rows = 2 * BLOCK * len(layout.entries)
    return pl.pallas_call(
        functools.partial(table_kernel, layout, ("outer", "inner")),
        out_shape=jax.ShapeDtypeStruct((rows, 128), jnp.float32),
        in_specs=[vmem],
        out_specs=vmem,
        compiler_params=pltpu.CompilerParams(vmem_limit_bytes=VMEM_BYTES),
        cost_estimate=pl.CostEstimate(
            flops=rows * 128 * 20, bytes_accessed=rows * 512, transcendentals=rows * 128
        ),
    )(jnp.asarray(lane_nodes()))


def run_levels(rows, table, layout):
    vmem = pl.BlockSpec(memory_space=pltpu.VMEM)
    return pl.pallas_call(
        functools.partial(level_kernel, layout),
        out_shape=jax.ShapeDtypeStruct(rows.shape, jnp.float32),
        in_specs=[vmem] * 3,
        out_specs=pl.BlockSpec(memory_space=pl.ANY),
        scratch_shapes=[pltpu.VMEM(rows.shape, jnp.float32), pltpu.SemaphoreType.DMA((8,))],
        compiler_params=pltpu.CompilerParams(vmem_limit_bytes=VMEM_BYTES),
    )(rows, table, jnp.asarray(split_matrices()))


def reorder_plan(plan, order):
    def place(bit):
        return bit if bit is None or isinstance(bit, tuple) else order.index(bit)

    return [
        (dimension, place(moved), [[place(b) for b in g] for g in target], [[place(b) for b in g] for g in source])
        for dimension, moved, target, source in plan
    ]


def reorder_rows(rows, order):
    count = len(order)
    if list(order) == list(range(count)):
        return rows
    axes = [count - 1 - order[count - 1 - i] for i in range(count)]
    return rows.reshape((2,) * count + (128,)).transpose(axes + [count]).reshape(rows.shape)


def level_groups(plan, row_bits):
    moved = [entry[1] for entry in plan[:-1]]
    groups = []
    level = 0
    while level < len(moved):
        count = min(len(moved) - level, row_bits - LOW_BITS)
        group = moved[level : level + count]
        order = [bit for bit in range(row_bits) if bit not in group] + sorted(group)
        groups.append((order, Layout(reorder_plan(plan[level : level + count + 1], order), row_bits)))
        level += count
    return groups


def body(weights):
    row_bits = weights.shape[0].bit_length() - 1
    inner_bits = lax.axis_size("inner").bit_length() - 1
    outer_bits = lax.axis_size("outer").bit_length() - 1
    groups = level_groups(level_plan(row_bits, inner_bits, outer_bits), row_bits)
    rows = lax.all_to_all(weights, ("inner", "outer"), 0, 0, tiled=True)
    tables = [rotations(layout) for _, layout in groups]
    for (order, layout), table in zip(groups, tables):
        rows = run_levels(reorder_rows(rows, order), table, layout)
        rows = reorder_rows(rows, [order.index(bit) for bit in range(row_bits)])
    return rows


def solution(mesh):
    spec = P(("outer", "inner"), None)
    return jax.shard_map(body, mesh=mesh, in_specs=(spec,), out_specs=spec, check_vma=False)
```

```python
import functools

import jax
import jax.numpy as jnp
import numpy as np
from jax import lax
from jax.experimental import pallas as pl
from jax.experimental.pallas import tpu as pltpu
from jax.sharding import PartitionSpec as P

GRID_N = 16384
TREE_LEVELS = 11
LOW_BITS = 3
BLOCK = 1 << LOW_BITS
VMEM_BYTES = 16 * 1024 * 1024
DOTS = 4


def chebyshev_nodes():
    return 0.5 * np.cos(np.pi * (2.0 * np.arange(8) + 1.0) / 16.0)


def lagrange_weights(which_child):
    node_values = chebyshev_nodes()
    targets = (node_values + which_child - 0.5) / 2.0
    weights_table = np.ones((8, 8))
    for anchor in range(8):
        for other_node in range(8):
            if other_node != anchor:
                weights_table[anchor, :] = (
                    weights_table[anchor, :]
                    * (targets - node_values[other_node])
                    / (node_values[anchor] - node_values[other_node])
                )
    return weights_table


def merge_matrix(dimension):
    merge_table = np.zeros((256, 128))
    for which_child in range(2):
        weights_table = lagrange_weights(which_child)
        if dimension == 0:
            block_table = np.kron(weights_table, np.eye(8))
        else:
            block_table = np.kron(np.eye(8), weights_table)
        for half in range(2):
            first = half * 128 + which_child * 64
            merge_table[first : first + 64, half * 64 : half * 64 + 64] = block_table.T
    return merge_table


def split_matrices():
    parts = []
    for dimension in range(2):
        exact = merge_matrix(dimension).astype(np.float32)
        high = exact.astype(jnp.bfloat16)
        low = (exact - high.astype(np.float32)).astype(jnp.bfloat16)
        parts.append(np.concatenate([high, low], 1))
    return np.stack(parts)


def lane_nodes():
    lanes = np.arange(128) % 64
    nodes = chebyshev_nodes()
    return np.stack([nodes[lanes // 8], nodes[lanes % 8]] + [np.zeros(128)] * 6).astype(np.float32)


def level_plan(local_bits, inner_bits, outer_bits):
    levels_total = inner_bits + outer_bits
    carried = [local_bits + level for level in range(levels_total)]
    moved = [
        local_bits - inner_bits + level
        if level < inner_bits
        else local_bits - levels_total + level - inner_bits
        for level in range(levels_total)
    ]
    source = [[], []]
    for level in range(levels_total):
        source[(level + 1) % 2].append(("carried", level))
    source[0] += [local_bits - 7, local_bits - 6, local_bits - 5]
    source[1] += [local_bits - 4, local_bits - 3, local_bits - 2, local_bits - 1]
    target = [[], []]
    for ordinal in range(local_bits - 7):
        target[ordinal % 2].append(ordinal)

    def place(bit):
        if isinstance(bit, tuple):
            return moved[bit[1]]
        if bit in moved:
            return (moved.index(bit),)
        return bit

    source = [[place(bit) for bit in group] for group in source]
    target = [[place(bit) for bit in group] for group in target]
    plan = []
    for level in range(levels_total):
        dimension = (level + 1) % 2
        plan.append(
            (dimension, moved[level], [list(g) for g in target], [list(g) for g in source])
        )
        source[dimension] = source[dimension][1:]
        target[dimension] = [moved[level]] + target[dimension]
    plan.append((None, None, [list(g) for g in target], [list(g) for g in source]))
    return plan


def box_span(source):
    return GRID_N * 2.0 ** (len(source) - TREE_LEVELS)


def reduced(turns):
    return turns - jnp.floor(turns + 0.5)


def odd_series(coefficients, near, square):
    total = coefficients[-1]
    for coefficient in coefficients[-2::-1]:
        total = total * square + coefficient
    return total * near


def sincos(turns):
    near = turns - lax.round(turns, lax.RoundingMethod.TO_NEAREST_EVEN)
    square = near * near
    sine = series(SINE, square) * near
    cosine = series(COSINE, square)
    return sine * cosine, 1.0 - sine * sine


def series(coefficients, square):
    total = coefficients[-1]
    for coefficient in coefficients[-2::-1]:
        total = total * square + coefficient
    return total


def fit(function, powers):
    grid = 0.25 * (1.0 - np.cos(np.pi * (np.arange(2000) + 0.5) / 2000))
    matrix = np.stack([grid**power for power in powers], 1)
    exact = np.sqrt(2.0) * function(np.pi * grid)
    weight = np.ones_like(grid)
    best = None
    for _ in range(100):
        scale = np.sqrt(weight)
        solved = np.linalg.lstsq(matrix * scale[:, None], exact * scale, rcond=None)[0]
        error = np.abs(matrix @ solved - exact)
        if best is None or error.max() < best[0]:
            best = (error.max(), solved)
        weight = weight * error
        weight = weight / weight.sum()
    return [float(v) for v in best[1]]


SINE = fit(np.sin, (1, 3, 5, 7, 9))
COSINE = fit(np.cos, (0, 2, 4, 6, 8))


def combos(bits):
    result = [{}]
    for bit in bits:
        result = [{**one, bit: value} for one in result for value in range(2)]
    return result


def pick(assignment, bits):
    return tuple(assignment[bit] for bit in bits)


class Layout:
    def __init__(self, plan, row_bits):
        self.plan = plan
        self.leading = list(range(row_bits - 1, LOW_BITS - 1, -1))
        self.moved = [entry[1] for entry in plan[:-1]]
        self.packed = self.moved + [None]
        self.entries = {}
        self.table_rows = 0
        for level, packed in enumerate(self.packed):
            free = self.free(level)
            for one in combos(free):
                for branch in range(2 if level < len(self.moved) else 1):
                    self.entries[level, pick(one, free), branch] = self.table_rows
                    self.table_rows += BLOCK if packed is None else 2 * BLOCK

    def free(self, level):
        return [bit for bit in self.leading if bit != self.packed[level]]

    def place(self, level, one, branch=0):
        first = self.entries[level, pick(one, self.free(level)), branch]
        return slice(first, first + BLOCK), slice(first + BLOCK, first + 2 * BLOCK)

    def row(self, assignment):
        return sum(assignment[bit] << bit for bit in self.leading if bit in assignment)


def table_kernel(layout, axes, node_ref, table_ref):
    plan = layout.plan
    device = lax.axis_index(axes[0]) * lax.axis_size(axes[1]) + lax.axis_index(axes[1])
    rows = lax.broadcasted_iota(jnp.int32, (BLOCK, 128), 0)
    lanes = lax.broadcasted_iota(jnp.int32, (BLOCK, 128), 1)
    half = jnp.where(lanes < 64, 0.0, 1.0)
    row_bit = [(rows >> bit & 1).astype(jnp.float32) for bit in range(LOW_BITS)]
    node = [jnp.broadcast_to(node_ref[d : d + 1, :], (BLOCK, 128)) for d in range(2)]

    def index_tile(places, packed):
        total = jnp.full((BLOCK, 128), 0.5, jnp.float32)
        scalar = None
        for ordinal, where in enumerate(places):
            weight = float(1 << ordinal)
            if isinstance(where, tuple):
                term = (device >> where[0] & 1).astype(jnp.float32) * weight
                scalar = term if scalar is None else scalar + term
            elif where == packed:
                total = total + half * weight
            elif where < LOW_BITS:
                total = total + row_bit[where] * weight
        return total if scalar is None else total + scalar

    def index_lead(places, assignment):
        return sum(
            float(1 << ordinal) * assignment[where]
            for ordinal, where in enumerate(places)
            if not isinstance(where, tuple) and where in assignment
        )

    def by_lead(places, level, function):
        bits = [w for w in places if not isinstance(w, tuple) and w in layout.free(level)]
        tile = index_tile(places, layout.packed[level])
        values = {pick(one, bits): function(tile + index_lead(places, one)) for one in combos(bits)}
        return lambda one: values[pick(one, bits)]

    def root(value):
        return value * lax.rsqrt(value)

    def store(level, one, branch, turns):
        sine, cosine = sincos(turns)
        for place, value in zip(layout.place(level, one, branch), (cosine, sine)):
            table_ref[place, :] = value

    for level, (dimension, _, target, source) in enumerate(plan):
        width = [2.0 ** (-len(source[d])) for d in range(2)]
        span = [box_span(source[d]) for d in range(2)]
        waves = [
            by_lead(source[d], level, lambda box, d=d: sincos((box + node[d]) * width[d]))
            for d in range(2)
        ]
        center = [
            by_lead(target[d], level, lambda box, d=d: box * span[d] - GRID_N / 2.0)
            for d in range(2)
        ]
        for one in combos(layout.free(level)):
            (sine_one, cosine_one), (sine_two, cosine_two) = (waves[d](one) for d in range(2))
            speed = [0.125 + sine_one * sine_two * 0.0625, 0.125 + cosine_one * cosine_two * 0.0625]
            square = [value * value for value in speed]
            k = [center[d](one) for d in range(2)]
            if level == len(plan) - 1:
                radius = root(square[0] * (k[0] * k[0]) + square[1] * (k[1] * k[1]))
                linear = node[0] * width[0] * k[0] + node[1] * width[1] * k[1]
                sine, cosine = sincos((radius - jnp.floor(radius)) + linear)
                table_ref[layout.place(level, one)[0], :] = jnp.where(lanes < 64, cosine, sine)
                continue
            other = 1 - dimension
            fixed = square[other] * (k[other] * k[other])
            radius = root(fixed + square[dimension] * (k[dimension] * k[dimension]))
            for branch in range(2):
                shift = (branch - 0.5) * 0.5 * span[dimension]
                child = k[dimension] + shift
                turns = root(fixed + square[dimension] * (child * child))
                if level > 0:
                    turns = (turns - radius) + node[dimension] * (width[dimension] * shift)
                else:
                    linear = node[dimension] * width[dimension] * child
                    linear = linear + node[other] * width[other] * k[other]
                    turns = (turns - jnp.floor(turns)) + linear
                store(level, one, branch, turns)


def level_kernel(layout, x_ref, table_ref, matrix_ref, out_ref, done_ref, sems):
    low_half = lax.broadcasted_iota(jnp.int32, (BLOCK, 128), 1) < 64
    last = len(layout.moved)

    def pack(first, second):
        return (
            jnp.where(low_half, first, pltpu.roll(second, 64, 1)),
            jnp.where(low_half, pltpu.roll(first, 64, 1), second),
        )

    state = {}
    for one in combos(layout.free(0)):
        halves = []
        for value in range(2):
            first = layout.row({**one, layout.packed[0]: value})
            halves.append(x_ref[first : first + BLOCK, :])
        state[pick(one, layout.free(0))] = pack(*halves)

    for level, moved in enumerate(layout.moved):
        free, packed = layout.free(level), layout.packed[level + 1]
        next_free = layout.free(level + 1)
        matrix = matrix_ref[layout.plan[level][0]]
        later = layout.packed[level + 1 :]
        order = sorted(
            (bit for bit in next_free if bit != moved),
            key=lambda bit: -later.index(bit) if bit in later else -99 * (bit not in layout.packed),
        )
        next_state = {}
        groups = combos(order)
        step = max(1, len(groups) // (DOTS if packed is not None else 8))
        for start in range(0, len(groups), step):
            parts = []
            places = []
            for group in groups[start : start + step]:
                halves = []
                for half in range(1 if packed is None else 2):
                    one = {**group, packed: half}
                    real, imaginary = state[pick(one, free)]
                    turned = []
                    for branch in range(2):
                        cosine, sine = (table_ref[place, :] for place in layout.place(level, one, branch))
                        turned.append((real * cosine - imaginary * sine, real * sine + imaginary * cosine))
                    halves.append(turned)
                if packed is None:
                    values = [jnp.concatenate([jnp.concatenate(pair, 1) for pair in halves[0]], 0)]
                else:
                    values = [
                        jnp.concatenate([jnp.concatenate(turned[branch], 0) for turned in halves], 1)
                        for branch in range(2)
                    ]
                tops = [value.astype(jnp.bfloat16) for value in values]
                parts += tops
                parts += [
                    (value - top.astype(jnp.float32)).astype(jnp.bfloat16)
                    for value, top in zip(values, tops)
                ]
                places += [pick({**group, moved: branch}, next_free) for branch in range(2)]
            product = jnp.dot(jnp.concatenate(parts, 0), matrix, preferred_element_type=jnp.float32)
            count = len(values)
            for index in range(len(parts) // 2):
                first = (index // count * 2 * count + index % count) * 2 * BLOCK
                top = product[first : first + 2 * BLOCK]
                rest = product[first + 2 * count * BLOCK : first + 2 * (count + 1) * BLOCK]
                total = (top[:, 128:] + rest[:, :128]) + top[:, :128]
                pair = total[:BLOCK], total[BLOCK:]
                if packed is None:
                    next_state[places[2 * index]], next_state[places[2 * index + 1]] = pair
                else:
                    next_state[places[index]] = pair
        state = next_state

    copies = []
    shared, lower = layout.leading[:3], layout.leading[3:]
    for one in combos(layout.leading):
        values = state[pick(one, layout.leading)]
        wave = table_ref[layout.place(last, one)[0], :]
        turned = pltpu.roll(wave, 64, 1)
        cosine, sine = jnp.where(low_half, wave, turned), jnp.where(low_half, turned, -wave)
        first = layout.row(one)
        done_ref[first : first + BLOCK, :] = values * cosine + pltpu.roll(values, 64, 1) * sine
        if all(one[bit] == 1 for bit in lower):
            piece = pl.ds(layout.row({bit: one[bit] for bit in shared}), BLOCK << len(lower))
            copy = pltpu.make_async_copy(done_ref.at[piece], out_ref.at[piece], sems.at[len(copies)])
            copy.start()
            copies.append(copy)
    for copy in copies:
        copy.wait()


def rotations(layout):
    vmem = pl.BlockSpec(memory_space=pltpu.VMEM)
    rows = layout.table_rows
    return pl.pallas_call(
        functools.partial(table_kernel, layout, ("outer", "inner")),
        out_shape=jax.ShapeDtypeStruct((rows, 128), jnp.float32),
        in_specs=[vmem],
        out_specs=vmem,
        compiler_params=pltpu.CompilerParams(vmem_limit_bytes=VMEM_BYTES),
        cost_estimate=pl.CostEstimate(
            flops=rows * 128 * 20, bytes_accessed=rows * 512, transcendentals=rows * 128
        ),
    )(jnp.asarray(lane_nodes()))


def run_levels(rows, table, layout):
    vmem = pl.BlockSpec(memory_space=pltpu.VMEM)
    return pl.pallas_call(
        functools.partial(level_kernel, layout),
        out_shape=jax.ShapeDtypeStruct(rows.shape, jnp.float32),
        in_specs=[vmem] * 3,
        out_specs=pl.BlockSpec(memory_space=pl.ANY),
        scratch_shapes=[pltpu.VMEM(rows.shape, jnp.float32), pltpu.SemaphoreType.DMA((8,))],
        compiler_params=pltpu.CompilerParams(vmem_limit_bytes=VMEM_BYTES),
    )(rows, table, jnp.asarray(split_matrices()))


def reorder_plan(plan, order):
    def place(bit):
        return bit if bit is None or isinstance(bit, tuple) else order.index(bit)

    return [
        (dimension, place(moved), [[place(b) for b in g] for g in target], [[place(b) for b in g] for g in source])
        for dimension, moved, target, source in plan
    ]


def reorder_rows(rows, order):
    count = len(order)
    if list(order) == list(range(count)):
        return rows
    axes = [count - 1 - order[count - 1 - i] for i in range(count)]
    return rows.reshape((2,) * count + (128,)).transpose(axes + [count]).reshape(rows.shape)


def level_groups(plan, row_bits):
    moved = [entry[1] for entry in plan[:-1]]
    groups = []
    level = 0
    while level < len(moved):
        count = min(len(moved) - level, row_bits - LOW_BITS)
        group = moved[level : level + count]
        order = [bit for bit in range(row_bits) if bit not in group] + sorted(group)
        groups.append((order, Layout(reorder_plan(plan[level : level + count + 1], order), row_bits)))
        level += count
    return groups


def body(weights):
    row_bits = weights.shape[0].bit_length() - 1
    inner_bits = lax.axis_size("inner").bit_length() - 1
    outer_bits = lax.axis_size("outer").bit_length() - 1
    groups = level_groups(level_plan(row_bits, inner_bits, outer_bits), row_bits)
    rows = lax.all_to_all(weights, ("inner", "outer"), 0, 0, tiled=True)
    tables = [rotations(layout) for _, layout in groups]
    for (order, layout), table in zip(groups, tables):
        rows = run_levels(reorder_rows(rows, order), table, layout)
        rows = reorder_rows(rows, [order.index(bit) for bit in range(row_bits)])
    return rows


def solution(mesh):
    spec = P(("outer", "inner"), None)
    return jax.shard_map(body, mesh=mesh, in_specs=(spec,), out_specs=spec, check_vma=False)
```

```python
import functools

import jax
import jax.numpy as jnp
import numpy as np
from jax import lax
from jax.experimental import pallas as pl
from jax.experimental.pallas import tpu as pltpu
from jax.sharding import PartitionSpec as P

GRID_N = 16384
TREE_LEVELS = 11
LOW_BITS = 3
BLOCK = 1 << LOW_BITS
VMEM_BYTES = 16 * 1024 * 1024
DOTS = 4


def chebyshev_nodes():
    return 0.5 * np.cos(np.pi * (2.0 * np.arange(8) + 1.0) / 16.0)


def lagrange_weights(which_child):
    node_values = chebyshev_nodes()
    targets = (node_values + which_child - 0.5) / 2.0
    weights_table = np.ones((8, 8))
    for anchor in range(8):
        for other_node in range(8):
            if other_node != anchor:
                weights_table[anchor, :] = (
                    weights_table[anchor, :]
                    * (targets - node_values[other_node])
                    / (node_values[anchor] - node_values[other_node])
                )
    return weights_table


def merge_matrix(dimension):
    merge_table = np.zeros((256, 128))
    for which_child in range(2):
        weights_table = lagrange_weights(which_child)
        if dimension == 0:
            block_table = np.kron(weights_table, np.eye(8))
        else:
            block_table = np.kron(np.eye(8), weights_table)
        for half in range(2):
            first = half * 128 + which_child * 64
            merge_table[first : first + 64, half * 64 : half * 64 + 64] = block_table.T
    return merge_table


def split_matrices():
    parts = []
    for dimension in range(2):
        exact = merge_matrix(dimension).astype(np.float32)
        high = exact.astype(jnp.bfloat16)
        low = (exact - high.astype(np.float32)).astype(jnp.bfloat16)
        parts.append(np.concatenate([high, low], 1))
    return np.stack(parts)


def lane_nodes():
    lanes = np.arange(128) % 64
    nodes = chebyshev_nodes()
    return np.stack([nodes[lanes // 8], nodes[lanes % 8]] + [np.zeros(128)] * 6).astype(np.float32)


def level_plan(local_bits, inner_bits, outer_bits):
    levels_total = inner_bits + outer_bits
    carried = [local_bits + level for level in range(levels_total)]
    moved = [
        local_bits - inner_bits + level
        if level < inner_bits
        else local_bits - levels_total + level - inner_bits
        for level in range(levels_total)
    ]
    source = [[], []]
    for level in range(levels_total):
        source[(level + 1) % 2].append(("carried", level))
    source[0] += [local_bits - 7, local_bits - 6, local_bits - 5]
    source[1] += [local_bits - 4, local_bits - 3, local_bits - 2, local_bits - 1]
    target = [[], []]
    for ordinal in range(local_bits - 7):
        target[ordinal % 2].append(ordinal)

    def place(bit):
        if isinstance(bit, tuple):
            return moved[bit[1]]
        if bit in moved:
            return (moved.index(bit),)
        return bit

    source = [[place(bit) for bit in group] for group in source]
    target = [[place(bit) for bit in group] for group in target]
    plan = []
    for level in range(levels_total):
        dimension = (level + 1) % 2
        plan.append(
            (dimension, moved[level], [list(g) for g in target], [list(g) for g in source])
        )
        source[dimension] = source[dimension][1:]
        target[dimension] = [moved[level]] + target[dimension]
    plan.append((None, None, [list(g) for g in target], [list(g) for g in source]))
    return plan


def box_span(source):
    return GRID_N * 2.0 ** (len(source) - TREE_LEVELS)


def reduced(turns):
    return turns - jnp.floor(turns + 0.5)


def odd_series(coefficients, near, square):
    total = coefficients[-1]
    for coefficient in coefficients[-2::-1]:
        total = total * square + coefficient
    return total * near


def sincos(turns):
    near = turns - lax.round(turns, lax.RoundingMethod.TO_NEAREST_EVEN)
    square = near * near
    sine = series(SINE, square) * near
    cosine = series(COSINE, square)
    return sine * cosine, 1.0 - sine * sine


def series(coefficients, square):
    total = coefficients[-1]
    for coefficient in coefficients[-2::-1]:
        total = total * square + coefficient
    return total


def fit(function, powers):
    grid = 0.25 * (1.0 - np.cos(np.pi * (np.arange(2000) + 0.5) / 2000))
    matrix = np.stack([grid**power for power in powers], 1)
    exact = np.sqrt(2.0) * function(np.pi * grid)
    weight = np.ones_like(grid)
    best = None
    for _ in range(100):
        scale = np.sqrt(weight)
        solved = np.linalg.lstsq(matrix * scale[:, None], exact * scale, rcond=None)[0]
        error = np.abs(matrix @ solved - exact)
        if best is None or error.max() < best[0]:
            best = (error.max(), solved)
        weight = weight * error
        weight = weight / weight.sum()
    return [float(v) for v in best[1]]


SINE = fit(np.sin, (1, 3, 5, 7, 9))
COSINE = fit(np.cos, (0, 2, 4, 6, 8))


def combos(bits):
    result = [{}]
    for bit in bits:
        result = [{**one, bit: value} for one in result for value in range(2)]
    return result


def pick(assignment, bits):
    return tuple(assignment[bit] for bit in bits)


class Layout:
    def __init__(self, plan, row_bits):
        self.plan = plan
        self.leading = list(range(row_bits - 1, LOW_BITS - 1, -1))
        self.moved = [entry[1] for entry in plan[:-1]]
        self.packed = self.moved + [[bit for bit in self.leading if bit != self.moved[-1]][0]]
        self.entries = {}
        for level, packed in enumerate(self.packed):
            free = self.free(level)
            for one in combos(free):
                for branch in range(2 if level < len(self.moved) else 1):
                    self.entries[level, pick(one, free), branch] = len(self.entries)

    def free(self, level):
        return [bit for bit in self.leading if bit != self.packed[level]]

    def place(self, level, one, branch=0):
        first = self.entries[level, pick(one, self.free(level)), branch] * 2 * BLOCK
        return slice(first, first + BLOCK), slice(first + BLOCK, first + 2 * BLOCK)

    def row(self, assignment):
        return sum(assignment[bit] << bit for bit in self.leading if bit in assignment)


def table_kernel(layout, axes, node_ref, table_ref):
    plan = layout.plan
    device = lax.axis_index(axes[0]) * lax.axis_size(axes[1]) + lax.axis_index(axes[1])
    rows = lax.broadcasted_iota(jnp.int32, (BLOCK, 128), 0)
    lanes = lax.broadcasted_iota(jnp.int32, (BLOCK, 128), 1)
    half = jnp.where(lanes < 64, 0.0, 1.0)
    row_bit = [(rows >> bit & 1).astype(jnp.float32) for bit in range(LOW_BITS)]
    node = [jnp.broadcast_to(node_ref[d : d + 1, :], (BLOCK, 128)) for d in range(2)]

    def index_tile(places, packed):
        total = jnp.full((BLOCK, 128), 0.5, jnp.float32)
        scalar = None
        for ordinal, where in enumerate(places):
            weight = float(1 << ordinal)
            if isinstance(where, tuple):
                term = (device >> where[0] & 1).astype(jnp.float32) * weight
                scalar = term if scalar is None else scalar + term
            elif where == packed:
                total = total + half * weight
            elif where < LOW_BITS:
                total = total + row_bit[where] * weight
        return total if scalar is None else total + scalar

    def index_lead(places, assignment):
        return sum(
            float(1 << ordinal) * assignment[where]
            for ordinal, where in enumerate(places)
            if not isinstance(where, tuple) and where in assignment
        )

    def by_lead(places, level, function):
        bits = [w for w in places if not isinstance(w, tuple) and w in layout.free(level)]
        tile = index_tile(places, layout.packed[level])
        values = {pick(one, bits): function(tile + index_lead(places, one)) for one in combos(bits)}
        return lambda one: values[pick(one, bits)]

    def root(value):
        return value * lax.rsqrt(value)

    def store(level, one, branch, turns):
        sine, cosine = sincos(turns)
        for place, value in zip(layout.place(level, one, branch), (cosine, sine)):
            table_ref[place, :] = value

    for level, (dimension, _, target, source) in enumerate(plan):
        width = [2.0 ** (-len(source[d])) for d in range(2)]
        span = [box_span(source[d]) for d in range(2)]
        waves = [
            by_lead(source[d], level, lambda box, d=d: sincos((box + node[d]) * width[d]))
            for d in range(2)
        ]
        center = [
            by_lead(target[d], level, lambda box, d=d: box * span[d] - GRID_N / 2.0)
            for d in range(2)
        ]
        for one in combos(layout.free(level)):
            (sine_one, cosine_one), (sine_two, cosine_two) = (waves[d](one) for d in range(2))
            speed = [0.125 + sine_one * sine_two * 0.0625, 0.125 + cosine_one * cosine_two * 0.0625]
            square = [value * value for value in speed]
            k = [center[d](one) for d in range(2)]
            if level == len(plan) - 1:
                radius = root(square[0] * (k[0] * k[0]) + square[1] * (k[1] * k[1]))
                linear = node[0] * width[0] * k[0] + node[1] * width[1] * k[1]
                store(level, one, 0, (radius - jnp.floor(radius)) + linear)
                continue
            other = 1 - dimension
            fixed = square[other] * (k[other] * k[other])
            radius = root(fixed + square[dimension] * (k[dimension] * k[dimension]))
            for branch in range(2):
                shift = (branch - 0.5) * 0.5 * span[dimension]
                child = k[dimension] + shift
                turns = root(fixed + square[dimension] * (child * child))
                if level > 0:
                    turns = (turns - radius) + node[dimension] * (width[dimension] * shift)
                else:
                    linear = node[dimension] * width[dimension] * child
                    linear = linear + node[other] * width[other] * k[other]
                    turns = (turns - jnp.floor(turns)) + linear
                store(level, one, branch, turns)


def level_kernel(layout, x_ref, table_ref, matrix_ref, out_ref, done_ref, sems):
    low_half = lax.broadcasted_iota(jnp.int32, (BLOCK, 128), 1) < 64
    last = len(layout.moved)

    def pack(first, second):
        crossed = pltpu.roll(jnp.where(low_half, second, first), 64, 1)
        return jnp.where(low_half, first, crossed), jnp.where(low_half, crossed, second)

    state = {}
    for one in combos(layout.free(0)):
        halves = []
        for value in range(2):
            first = layout.row({**one, layout.packed[0]: value})
            halves.append(x_ref[first : first + BLOCK, :])
        state[pick(one, layout.free(0))] = pack(*halves)

    for level, moved in enumerate(layout.moved):
        free, packed = layout.free(level), layout.packed[level + 1]
        next_free = layout.free(level + 1)
        matrix = matrix_ref[layout.plan[level][0]]
        later = layout.packed[level + 1 :]
        order = sorted(
            (bit for bit in next_free if bit != moved),
            key=lambda bit: -later.index(bit) if bit in later else -99 * (bit not in layout.packed),
        )
        next_state = {}
        groups = combos(order)
        step = max(1, len(groups) // DOTS)
        for start in range(0, len(groups), step):
            parts = []
            places = []
            for group in groups[start : start + step]:
                halves = []
                for half in range(2):
                    one = {**group, packed: half}
                    real, imaginary = state[pick(one, free)]
                    turned = []
                    for branch in range(2):
                        cosine, sine = (table_ref[place, :] for place in layout.place(level, one, branch))
                        both = (real * cosine - imaginary * sine, real * sine + imaginary * cosine)
                        turned.append(jnp.concatenate(both, 0))
                    halves.append(turned)
                values = [jnp.concatenate([turned[branch] for turned in halves], 1) for branch in range(2)]
                tops = [value.astype(jnp.bfloat16) for value in values]
                parts += tops
                parts += [
                    (value - top.astype(jnp.float32)).astype(jnp.bfloat16)
                    for value, top in zip(values, tops)
                ]
                places += [pick({**group, moved: branch}, next_free) for branch in range(2)]
            product = jnp.dot(jnp.concatenate(parts, 0), matrix, preferred_element_type=jnp.float32)
            for index, place in enumerate(places):
                first = (index // 2 * 4 + index % 2) * 2 * BLOCK
                top = product[first : first + 2 * BLOCK]
                rest = product[first + 4 * BLOCK : first + 6 * BLOCK]
                total = (top[:, 128:] + rest[:, :128]) + top[:, :128]
                next_state[place] = (total[:BLOCK], total[BLOCK:])
        state = next_state

    packed, free = layout.packed[last], layout.free(last)
    copies = []
    for one in combos(free):
        real, imaginary = state[pick(one, free)]
        cosine, sine = (table_ref[place, :] for place in layout.place(last, one))
        outputs = pack(real * cosine + imaginary * sine, imaginary * cosine - real * sine)
        for value in range(2):
            first = layout.row({**one, packed: value})
            done_ref[first : first + BLOCK, :] = outputs[value]
        if all(one[bit] == 1 for bit in free[2:]):
            for value in range(2):
                shared = {bit: one[bit] for bit in free[:2]}
                piece = pl.ds(layout.row({**shared, packed: value}), BLOCK << len(free) - 2)
                copy = pltpu.make_async_copy(done_ref.at[piece], out_ref.at[piece], sems.at[len(copies)])
                copy.start()
                copies.append(copy)
    for copy in copies:
        copy.wait()


def rotations(layout):
    vmem = pl.BlockSpec(memory_space=pltpu.VMEM)
    rows = 2 * BLOCK * len(layout.entries)
    return pl.pallas_call(
        functools.partial(table_kernel, layout, ("outer", "inner")),
        out_shape=jax.ShapeDtypeStruct((rows, 128), jnp.float32),
        in_specs=[vmem],
        out_specs=vmem,
        compiler_params=pltpu.CompilerParams(vmem_limit_bytes=VMEM_BYTES),
        cost_estimate=pl.CostEstimate(
            flops=rows * 128 * 20, bytes_accessed=rows * 512, transcendentals=rows * 128
        ),
    )(jnp.asarray(lane_nodes()))


def run_levels(rows, table, layout):
    vmem = pl.BlockSpec(memory_space=pltpu.VMEM)
    return pl.pallas_call(
        functools.partial(level_kernel, layout),
        out_shape=jax.ShapeDtypeStruct(rows.shape, jnp.float32),
        in_specs=[vmem] * 3,
        out_specs=pl.BlockSpec(memory_space=pl.ANY),
        scratch_shapes=[pltpu.VMEM(rows.shape, jnp.float32), pltpu.SemaphoreType.DMA((8,))],
        compiler_params=pltpu.CompilerParams(vmem_limit_bytes=VMEM_BYTES),
    )(rows, table, jnp.asarray(split_matrices()))


def reorder_plan(plan, order):
    def place(bit):
        return bit if bit is None or isinstance(bit, tuple) else order.index(bit)

    return [
        (dimension, place(moved), [[place(b) for b in g] for g in target], [[place(b) for b in g] for g in source])
        for dimension, moved, target, source in plan
    ]


def reorder_rows(rows, order):
    count = len(order)
    if list(order) == list(range(count)):
        return rows
    axes = [count - 1 - order[count - 1 - i] for i in range(count)]
    return rows.reshape((2,) * count + (128,)).transpose(axes + [count]).reshape(rows.shape)


def level_groups(plan, row_bits):
    moved = [entry[1] for entry in plan[:-1]]
    groups = []
    level = 0
    while level < len(moved):
        count = min(len(moved) - level, row_bits - LOW_BITS)
        group = moved[level : level + count]
        order = [bit for bit in range(row_bits) if bit not in group] + sorted(group)
        groups.append((order, Layout(reorder_plan(plan[level : level + count + 1], order), row_bits)))
        level += count
    return groups


def body(weights):
    row_bits = weights.shape[0].bit_length() - 1
    inner_bits = lax.axis_size("inner").bit_length() - 1
    outer_bits = lax.axis_size("outer").bit_length() - 1
    groups = level_groups(level_plan(row_bits, inner_bits, outer_bits), row_bits)
    rows = lax.all_to_all(weights, ("inner", "outer"), 0, 0, tiled=True)
    tables = [rotations(layout) for _, layout in groups]
    for (order, layout), table in zip(groups, tables):
        rows = run_levels(reorder_rows(rows, order), table, layout)
        rows = reorder_rows(rows, [order.index(bit) for bit in range(row_bits)])
    return rows


def solution(mesh):
    spec = P(("outer", "inner"), None)
    return jax.shard_map(body, mesh=mesh, in_specs=(spec,), out_specs=spec, check_vma=False)
```

```python
import functools

import jax
import jax.numpy as jnp
import numpy as np
from jax import lax
from jax.experimental import pallas as pl
from jax.experimental.pallas import tpu as pltpu
from jax.sharding import PartitionSpec as P

GRID_N = 16384
TREE_LEVELS = 11
LOW_BITS = 3
BLOCK = 1 << LOW_BITS
VMEM_BYTES = 16 * 1024 * 1024
DOTS = 2


def chebyshev_nodes():
    return 0.5 * np.cos(np.pi * (2.0 * np.arange(8) + 1.0) / 16.0)


def lagrange_weights(which_child):
    node_values = chebyshev_nodes()
    targets = (node_values + which_child - 0.5) / 2.0
    weights_table = np.ones((8, 8))
    for anchor in range(8):
        for other_node in range(8):
            if other_node != anchor:
                weights_table[anchor, :] = (
                    weights_table[anchor, :]
                    * (targets - node_values[other_node])
                    / (node_values[anchor] - node_values[other_node])
                )
    return weights_table


def merge_matrix(dimension):
    merge_table = np.zeros((256, 128))
    for which_child in range(2):
        weights_table = lagrange_weights(which_child)
        if dimension == 0:
            block_table = np.kron(weights_table, np.eye(8))
        else:
            block_table = np.kron(np.eye(8), weights_table)
        for half in range(2):
            first = half * 128 + which_child * 64
            merge_table[first : first + 64, half * 64 : half * 64 + 64] = block_table.T
    return merge_table


def split_matrices():
    parts = []
    for dimension in range(2):
        exact = merge_matrix(dimension).astype(np.float32)
        high = exact.astype(jnp.bfloat16)
        low = (exact - high.astype(np.float32)).astype(jnp.bfloat16)
        parts.append(np.concatenate([high, low], 1))
    return np.stack(parts)


def lane_nodes():
    lanes = np.arange(128) % 64
    nodes = chebyshev_nodes()
    return np.stack([nodes[lanes // 8], nodes[lanes % 8]] + [np.zeros(128)] * 6).astype(np.float32)


def level_plan(local_bits, inner_bits, outer_bits):
    levels_total = inner_bits + outer_bits
    carried = [local_bits + level for level in range(levels_total)]
    moved = [
        local_bits - inner_bits + level
        if level < inner_bits
        else local_bits - levels_total + level - inner_bits
        for level in range(levels_total)
    ]
    source = [[], []]
    for level in range(levels_total):
        source[(level + 1) % 2].append(("carried", level))
    source[0] += [local_bits - 7, local_bits - 6, local_bits - 5]
    source[1] += [local_bits - 4, local_bits - 3, local_bits - 2, local_bits - 1]
    target = [[], []]
    for ordinal in range(local_bits - 7):
        target[ordinal % 2].append(ordinal)

    def place(bit):
        if isinstance(bit, tuple):
            return moved[bit[1]]
        if bit in moved:
            return (moved.index(bit),)
        return bit

    source = [[place(bit) for bit in group] for group in source]
    target = [[place(bit) for bit in group] for group in target]
    plan = []
    for level in range(levels_total):
        dimension = (level + 1) % 2
        plan.append(
            (dimension, moved[level], [list(g) for g in target], [list(g) for g in source])
        )
        source[dimension] = source[dimension][1:]
        target[dimension] = [moved[level]] + target[dimension]
    plan.append((None, None, [list(g) for g in target], [list(g) for g in source]))
    return plan


def box_span(source):
    return GRID_N * 2.0 ** (len(source) - TREE_LEVELS)


def reduced(turns):
    return turns - jnp.floor(turns + 0.5)


def odd_series(coefficients, near, square):
    total = coefficients[-1]
    for coefficient in coefficients[-2::-1]:
        total = total * square + coefficient
    return total * near


def sincos(turns):
    near = turns - lax.round(turns, lax.RoundingMethod.TO_NEAREST_EVEN)
    square = near * near
    sine = series(SINE, square) * near
    cosine = series(COSINE, square)
    return sine * cosine, 1.0 - sine * sine


def series(coefficients, square):
    total = coefficients[-1]
    for coefficient in coefficients[-2::-1]:
        total = total * square + coefficient
    return total


def fit(function, powers):
    grid = 0.25 * (1.0 - np.cos(np.pi * (np.arange(2000) + 0.5) / 2000))
    matrix = np.stack([grid**power for power in powers], 1)
    exact = np.sqrt(2.0) * function(np.pi * grid)
    weight = np.ones_like(grid)
    best = None
    for _ in range(100):
        scale = np.sqrt(weight)
        solved = np.linalg.lstsq(matrix * scale[:, None], exact * scale, rcond=None)[0]
        error = np.abs(matrix @ solved - exact)
        if best is None or error.max() < best[0]:
            best = (error.max(), solved)
        weight = weight * error
        weight = weight / weight.sum()
    return [float(v) for v in best[1]]


SINE = fit(np.sin, (1, 3, 5, 7, 9))
COSINE = fit(np.cos, (0, 2, 4, 6, 8))


def combos(bits):
    result = [{}]
    for bit in bits:
        result = [{**one, bit: value} for one in result for value in range(2)]
    return result


def pick(assignment, bits):
    return tuple(assignment[bit] for bit in bits)


class Layout:
    def __init__(self, plan, row_bits):
        self.plan = plan
        self.leading = list(range(row_bits - 1, LOW_BITS - 1, -1))
        self.moved = [entry[1] for entry in plan[:-1]]
        self.packed = self.moved + [[bit for bit in self.leading if bit != self.moved[-1]][0]]
        self.entries = {}
        for level, packed in enumerate(self.packed):
            free = self.free(level)
            for one in combos(free):
                for branch in range(2 if level < len(self.moved) else 1):
                    self.entries[level, pick(one, free), branch] = len(self.entries)

    def free(self, level):
        return [bit for bit in self.leading if bit != self.packed[level]]

    def place(self, level, one, branch=0):
        first = self.entries[level, pick(one, self.free(level)), branch] * 2 * BLOCK
        return slice(first, first + BLOCK), slice(first + BLOCK, first + 2 * BLOCK)

    def row(self, assignment):
        return sum(assignment[bit] << bit for bit in self.leading if bit in assignment)


def table_kernel(layout, axes, node_ref, table_ref):
    plan = layout.plan
    device = lax.axis_index(axes[0]) * lax.axis_size(axes[1]) + lax.axis_index(axes[1])
    rows = lax.broadcasted_iota(jnp.int32, (BLOCK, 128), 0)
    lanes = lax.broadcasted_iota(jnp.int32, (BLOCK, 128), 1)
    half = jnp.where(lanes < 64, 0.0, 1.0)
    row_bit = [(rows >> bit & 1).astype(jnp.float32) for bit in range(LOW_BITS)]
    node = [jnp.broadcast_to(node_ref[d : d + 1, :], (BLOCK, 128)) for d in range(2)]

    def index_tile(places, packed):
        total = jnp.full((BLOCK, 128), 0.5, jnp.float32)
        scalar = None
        for ordinal, where in enumerate(places):
            weight = float(1 << ordinal)
            if isinstance(where, tuple):
                term = (device >> where[0] & 1).astype(jnp.float32) * weight
                scalar = term if scalar is None else scalar + term
            elif where == packed:
                total = total + half * weight
            elif where < LOW_BITS:
                total = total + row_bit[where] * weight
        return total if scalar is None else total + scalar

    def index_lead(places, assignment):
        return sum(
            float(1 << ordinal) * assignment[where]
            for ordinal, where in enumerate(places)
            if not isinstance(where, tuple) and where in assignment
        )

    def by_lead(places, level, function):
        bits = [w for w in places if not isinstance(w, tuple) and w in layout.free(level)]
        tile = index_tile(places, layout.packed[level])
        values = {pick(one, bits): function(tile + index_lead(places, one)) for one in combos(bits)}
        return lambda one: values[pick(one, bits)]

    def root(value):
        return value * lax.rsqrt(value)

    def store(level, one, branch, turns):
        sine, cosine = sincos(turns)
        for place, value in zip(layout.place(level, one, branch), (cosine, sine)):
            table_ref[place, :] = value

    for level, (dimension, _, target, source) in enumerate(plan):
        width = [2.0 ** (-len(source[d])) for d in range(2)]
        span = [box_span(source[d]) for d in range(2)]
        waves = [
            by_lead(source[d], level, lambda box, d=d: sincos((box + node[d]) * width[d]))
            for d in range(2)
        ]
        center = [
            by_lead(target[d], level, lambda box, d=d: box * span[d] - GRID_N / 2.0)
            for d in range(2)
        ]
        for one in combos(layout.free(level)):
            (sine_one, cosine_one), (sine_two, cosine_two) = (waves[d](one) for d in range(2))
            speed = [0.125 + sine_one * sine_two * 0.0625, 0.125 + cosine_one * cosine_two * 0.0625]
            square = [value * value for value in speed]
            k = [center[d](one) for d in range(2)]
            if level == len(plan) - 1:
                radius = root(square[0] * (k[0] * k[0]) + square[1] * (k[1] * k[1]))
                linear = node[0] * width[0] * k[0] + node[1] * width[1] * k[1]
                store(level, one, 0, (radius - jnp.floor(radius)) + linear)
                continue
            other = 1 - dimension
            fixed = square[other] * (k[other] * k[other])
            radius = root(fixed + square[dimension] * (k[dimension] * k[dimension]))
            for branch in range(2):
                shift = (branch - 0.5) * 0.5 * span[dimension]
                child = k[dimension] + shift
                turns = root(fixed + square[dimension] * (child * child))
                if level > 0:
                    turns = (turns - radius) + node[dimension] * (width[dimension] * shift)
                else:
                    linear = node[dimension] * width[dimension] * child
                    linear = linear + node[other] * width[other] * k[other]
                    turns = (turns - jnp.floor(turns)) + linear
                store(level, one, branch, turns)


def level_kernel(layout, x_ref, table_ref, matrix_ref, out_ref, done_ref, sems):
    low_half = lax.broadcasted_iota(jnp.int32, (BLOCK, 128), 1) < 64
    last = len(layout.moved)

    def pack(first, second):
        crossed = pltpu.roll(jnp.where(low_half, second, first), 64, 1)
        return jnp.where(low_half, first, crossed), jnp.where(low_half, crossed, second)

    state = {}
    for one in combos(layout.free(0)):
        halves = []
        for value in range(2):
            first = layout.row({**one, layout.packed[0]: value})
            halves.append(x_ref[first : first + BLOCK, :])
        state[pick(one, layout.free(0))] = pack(*halves)

    for level, moved in enumerate(layout.moved):
        free, packed = layout.free(level), layout.packed[level + 1]
        next_free = layout.free(level + 1)
        matrix = matrix_ref[layout.plan[level][0]]
        later = layout.packed[level + 1 :]
        order = sorted(
            (bit for bit in next_free if bit != moved),
            key=lambda bit: -later.index(bit) if bit in later else -99 * (bit not in layout.packed),
        )
        next_state = {}
        groups = combos(order)
        step = max(1, len(groups) // DOTS)
        for start in range(0, len(groups), step):
            parts = [[], []]
            places = []
            for group in groups[start : start + step]:
                halves = []
                for half in range(2):
                    one = {**group, packed: half}
                    real, imaginary = state[pick(one, free)]
                    turned = []
                    for branch in range(2):
                        cosine, sine = (table_ref[place, :] for place in layout.place(level, one, branch))
                        both = (real * cosine - imaginary * sine, real * sine + imaginary * cosine)
                        turned.append(jnp.concatenate(both, 0))
                    halves.append(turned)
                values = [jnp.concatenate([turned[branch] for turned in halves], 1) for branch in range(2)]
                tops = [value.astype(jnp.bfloat16) for value in values]
                parts[0] += tops
                parts[1] += [
                    (value - top.astype(jnp.float32))
                    for value, top in zip(values, tops)
                ]
                places += [pick({**group, moved: branch}, next_free) for branch in range(2)]
            tops = jnp.dot(jnp.concatenate(parts[0], 0), matrix, preferred_element_type=jnp.float32)
            rests = jnp.dot(jnp.concatenate(parts[1], 0), matrix[:, :128].astype(jnp.float32), preferred_element_type=jnp.float32)
            for index, place in enumerate(places):
                first = index * 2 * BLOCK
                top, rest = tops[first : first + 2 * BLOCK], rests[first : first + 2 * BLOCK]
                total = (top[:, 128:] + rest) + top[:, :128]
                next_state[place] = (total[:BLOCK], total[BLOCK:])
        state = next_state

    packed, free = layout.packed[last], layout.free(last)
    copies = []
    for one in combos(free):
        real, imaginary = state[pick(one, free)]
        cosine, sine = (table_ref[place, :] for place in layout.place(last, one))
        outputs = pack(real * cosine + imaginary * sine, imaginary * cosine - real * sine)
        for value in range(2):
            first = layout.row({**one, packed: value})
            done_ref[first : first + BLOCK, :] = outputs[value]
        if all(one[bit] == 1 for bit in free[2:]):
            for value in range(2):
                shared = {bit: one[bit] for bit in free[:2]}
                piece = pl.ds(layout.row({**shared, packed: value}), BLOCK << len(free) - 2)
                copy = pltpu.make_async_copy(done_ref.at[piece], out_ref.at[piece], sems.at[len(copies)])
                copy.start()
                copies.append(copy)
    for copy in copies:
        copy.wait()


def rotations(layout):
    vmem = pl.BlockSpec(memory_space=pltpu.VMEM)
    rows = 2 * BLOCK * len(layout.entries)
    return pl.pallas_call(
        functools.partial(table_kernel, layout, ("outer", "inner")),
        out_shape=jax.ShapeDtypeStruct((rows, 128), jnp.float32),
        in_specs=[vmem],
        out_specs=vmem,
        compiler_params=pltpu.CompilerParams(vmem_limit_bytes=VMEM_BYTES),
        cost_estimate=pl.CostEstimate(
            flops=rows * 128 * 20, bytes_accessed=rows * 512, transcendentals=rows * 128
        ),
    )(jnp.asarray(lane_nodes()))


def run_levels(rows, table, layout):
    vmem = pl.BlockSpec(memory_space=pltpu.VMEM)
    return pl.pallas_call(
        functools.partial(level_kernel, layout),
        out_shape=jax.ShapeDtypeStruct(rows.shape, jnp.float32),
        in_specs=[vmem] * 3,
        out_specs=pl.BlockSpec(memory_space=pl.ANY),
        scratch_shapes=[pltpu.VMEM(rows.shape, jnp.float32), pltpu.SemaphoreType.DMA((8,))],
        compiler_params=pltpu.CompilerParams(vmem_limit_bytes=VMEM_BYTES),
    )(rows, table, jnp.asarray(split_matrices()))


def reorder_plan(plan, order):
    def place(bit):
        return bit if bit is None or isinstance(bit, tuple) else order.index(bit)

    return [
        (dimension, place(moved), [[place(b) for b in g] for g in target], [[place(b) for b in g] for g in source])
        for dimension, moved, target, source in plan
    ]


def reorder_rows(rows, order):
    count = len(order)
    if list(order) == list(range(count)):
        return rows
    axes = [count - 1 - order[count - 1 - i] for i in range(count)]
    return rows.reshape((2,) * count + (128,)).transpose(axes + [count]).reshape(rows.shape)


def level_groups(plan, row_bits):
    moved = [entry[1] for entry in plan[:-1]]
    groups = []
    level = 0
    while level < len(moved):
        count = min(len(moved) - level, row_bits - LOW_BITS)
        group = moved[level : level + count]
        order = [bit for bit in range(row_bits) if bit not in group] + sorted(group)
        groups.append((order, Layout(reorder_plan(plan[level : level + count + 1], order), row_bits)))
        level += count
    return groups


def body(weights):
    row_bits = weights.shape[0].bit_length() - 1
    inner_bits = lax.axis_size("inner").bit_length() - 1
    outer_bits = lax.axis_size("outer").bit_length() - 1
    groups = level_groups(level_plan(row_bits, inner_bits, outer_bits), row_bits)
    rows = lax.all_to_all(weights, ("inner", "outer"), 0, 0, tiled=True)
    tables = [rotations(layout) for _, layout in groups]
    for (order, layout), table in zip(groups, tables):
        rows = run_levels(reorder_rows(rows, order), table, layout)
        rows = reorder_rows(rows, [order.index(bit) for bit in range(row_bits)])
    return rows


def solution(mesh):
    spec = P(("outer", "inner"), None)
    return jax.shard_map(body, mesh=mesh, in_specs=(spec,), out_specs=spec, check_vma=False)
```

```python
import functools

import jax
import jax.numpy as jnp
import numpy as np
from jax import lax
from jax.experimental import pallas as pl
from jax.experimental.pallas import tpu as pltpu
from jax.sharding import PartitionSpec as P

GRID_N = 16384
TREE_LEVELS = 11
LOW_BITS = 3
BLOCK = 1 << LOW_BITS
VMEM_BYTES = 16 * 1024 * 1024
DOTS = 2


def chebyshev_nodes():
    return 0.5 * np.cos(np.pi * (2.0 * np.arange(8) + 1.0) / 16.0)


def lagrange_weights(which_child):
    node_values = chebyshev_nodes()
    targets = (node_values + which_child - 0.5) / 2.0
    weights_table = np.ones((8, 8))
    for anchor in range(8):
        for other_node in range(8):
            if other_node != anchor:
                weights_table[anchor, :] = (
                    weights_table[anchor, :]
                    * (targets - node_values[other_node])
                    / (node_values[anchor] - node_values[other_node])
                )
    return weights_table


def merge_matrix(dimension):
    merge_table = np.zeros((256, 128))
    for which_child in range(2):
        weights_table = lagrange_weights(which_child)
        if dimension == 0:
            block_table = np.kron(weights_table, np.eye(8))
        else:
            block_table = np.kron(np.eye(8), weights_table)
        for half in range(2):
            first = half * 128 + which_child * 64
            merge_table[first : first + 64, half * 64 : half * 64 + 64] = block_table.T
    return merge_table


def split_matrices():
    parts = []
    for dimension in range(2):
        exact = merge_matrix(dimension).astype(np.float32)
        high = exact.astype(jnp.bfloat16)
        low = (exact - high.astype(np.float32)).astype(jnp.bfloat16)
        parts.append(np.concatenate([high, low], 1))
    return np.stack(parts)


def lane_nodes():
    lanes = np.arange(128) % 64
    nodes = chebyshev_nodes()
    return np.stack([nodes[lanes // 8], nodes[lanes % 8]] + [np.zeros(128)] * 6).astype(np.float32)


def level_plan(local_bits, inner_bits, outer_bits):
    levels_total = inner_bits + outer_bits
    carried = [local_bits + level for level in range(levels_total)]
    moved = [
        local_bits - inner_bits + level
        if level < inner_bits
        else local_bits - levels_total + level - inner_bits
        for level in range(levels_total)
    ]
    source = [[], []]
    for level in range(levels_total):
        source[(level + 1) % 2].append(("carried", level))
    source[0] += [local_bits - 7, local_bits - 6, local_bits - 5]
    source[1] += [local_bits - 4, local_bits - 3, local_bits - 2, local_bits - 1]
    target = [[], []]
    for ordinal in range(local_bits - 7):
        target[ordinal % 2].append(ordinal)

    def place(bit):
        if isinstance(bit, tuple):
            return moved[bit[1]]
        if bit in moved:
            return (moved.index(bit),)
        return bit

    source = [[place(bit) for bit in group] for group in source]
    target = [[place(bit) for bit in group] for group in target]
    plan = []
    for level in range(levels_total):
        dimension = (level + 1) % 2
        plan.append(
            (dimension, moved[level], [list(g) for g in target], [list(g) for g in source])
        )
        source[dimension] = source[dimension][1:]
        target[dimension] = [moved[level]] + target[dimension]
    plan.append((None, None, [list(g) for g in target], [list(g) for g in source]))
    return plan


def box_span(source):
    return GRID_N * 2.0 ** (len(source) - TREE_LEVELS)


def reduced(turns):
    return turns - jnp.floor(turns + 0.5)


def odd_series(coefficients, near, square):
    total = coefficients[-1]
    for coefficient in coefficients[-2::-1]:
        total = total * square + coefficient
    return total * near


def sincos(turns):
    near = turns - lax.round(turns, lax.RoundingMethod.TO_NEAREST_EVEN)
    square = near * near
    sine = series(SINE, square) * near
    cosine = series(COSINE, square)
    return sine * cosine, 1.0 - sine * sine


def series(coefficients, square):
    total = coefficients[-1]
    for coefficient in coefficients[-2::-1]:
        total = total * square + coefficient
    return total


def fit(function, powers):
    grid = 0.25 * (1.0 - np.cos(np.pi * (np.arange(2000) + 0.5) / 2000))
    matrix = np.stack([grid**power for power in powers], 1)
    exact = np.sqrt(2.0) * function(np.pi * grid)
    weight = np.ones_like(grid)
    best = None
    for _ in range(100):
        scale = np.sqrt(weight)
        solved = np.linalg.lstsq(matrix * scale[:, None], exact * scale, rcond=None)[0]
        error = np.abs(matrix @ solved - exact)
        if best is None or error.max() < best[0]:
            best = (error.max(), solved)
        weight = weight * error
        weight = weight / weight.sum()
    return [float(v) for v in best[1]]


SINE = fit(np.sin, (1, 3, 5, 7, 9))
COSINE = fit(np.cos, (0, 2, 4, 6, 8))


def combos(bits):
    result = [{}]
    for bit in bits:
        result = [{**one, bit: value} for one in result for value in range(2)]
    return result


def pick(assignment, bits):
    return tuple(assignment[bit] for bit in bits)


class Layout:
    def __init__(self, plan, row_bits):
        self.plan = plan
        self.leading = list(range(row_bits - 1, LOW_BITS - 1, -1))
        self.moved = [entry[1] for entry in plan[:-1]]
        self.packed = self.moved + [[bit for bit in self.leading if bit != self.moved[-1]][0]]
        self.entries = {}
        for level, packed in enumerate(self.packed):
            free = self.free(level)
            for one in combos(free):
                for branch in range(2 if level < len(self.moved) else 1):
                    self.entries[level, pick(one, free), branch] = len(self.entries)

    def free(self, level):
        return [bit for bit in self.leading if bit != self.packed[level]]

    def place(self, level, one, branch=0):
        first = self.entries[level, pick(one, self.free(level)), branch] * 2 * BLOCK
        return slice(first, first + BLOCK), slice(first + BLOCK, first + 2 * BLOCK)

    def row(self, assignment):
        return sum(assignment[bit] << bit for bit in self.leading if bit in assignment)


def table_kernel(layout, axes, node_ref, table_ref):
    plan = layout.plan
    device = lax.axis_index(axes[0]) * lax.axis_size(axes[1]) + lax.axis_index(axes[1])
    rows = lax.broadcasted_iota(jnp.int32, (BLOCK, 128), 0)
    lanes = lax.broadcasted_iota(jnp.int32, (BLOCK, 128), 1)
    half = jnp.where(lanes < 64, 0.0, 1.0)
    row_bit = [(rows >> bit & 1).astype(jnp.float32) for bit in range(LOW_BITS)]
    node = [jnp.broadcast_to(node_ref[d : d + 1, :], (BLOCK, 128)) for d in range(2)]

    def index_tile(places, packed):
        total = jnp.full((BLOCK, 128), 0.5, jnp.float32)
        scalar = None
        for ordinal, where in enumerate(places):
            weight = float(1 << ordinal)
            if isinstance(where, tuple):
                term = (device >> where[0] & 1).astype(jnp.float32) * weight
                scalar = term if scalar is None else scalar + term
            elif where == packed:
                total = total + half * weight
            elif where < LOW_BITS:
                total = total + row_bit[where] * weight
        return total if scalar is None else total + scalar

    def index_lead(places, assignment):
        return sum(
            float(1 << ordinal) * assignment[where]
            for ordinal, where in enumerate(places)
            if not isinstance(where, tuple) and where in assignment
        )

    def by_lead(places, level, function):
        bits = [w for w in places if not isinstance(w, tuple) and w in layout.free(level)]
        tile = index_tile(places, layout.packed[level])
        values = {pick(one, bits): function(tile + index_lead(places, one)) for one in combos(bits)}
        return lambda one: values[pick(one, bits)]

    def root(value):
        return value * lax.rsqrt(value)

    def store(level, one, branch, turns):
        sine, cosine = sincos(turns)
        for place, value in zip(layout.place(level, one, branch), (cosine, sine)):
            table_ref[place, :] = value

    for level, (dimension, _, target, source) in enumerate(plan):
        width = [2.0 ** (-len(source[d])) for d in range(2)]
        span = [box_span(source[d]) for d in range(2)]
        waves = [
            by_lead(source[d], level, lambda box, d=d: sincos((box + node[d]) * width[d]))
            for d in range(2)
        ]
        center = [
            by_lead(target[d], level, lambda box, d=d: box * span[d] - GRID_N / 2.0)
            for d in range(2)
        ]
        for one in combos(layout.free(level)):
            (sine_one, cosine_one), (sine_two, cosine_two) = (waves[d](one) for d in range(2))
            speed = [0.125 + sine_one * sine_two * 0.0625, 0.125 + cosine_one * cosine_two * 0.0625]
            square = [value * value for value in speed]
            k = [center[d](one) for d in range(2)]
            if level == len(plan) - 1:
                radius = root(square[0] * (k[0] * k[0]) + square[1] * (k[1] * k[1]))
                linear = node[0] * width[0] * k[0] + node[1] * width[1] * k[1]
                store(level, one, 0, (radius - jnp.floor(radius)) + linear)
                continue
            other = 1 - dimension
            fixed = square[other] * (k[other] * k[other])
            radius = root(fixed + square[dimension] * (k[dimension] * k[dimension]))
            for branch in range(2):
                shift = (branch - 0.5) * 0.5 * span[dimension]
                child = k[dimension] + shift
                turns = root(fixed + square[dimension] * (child * child))
                if level > 0:
                    turns = (turns - radius) + node[dimension] * (width[dimension] * shift)
                else:
                    linear = node[dimension] * width[dimension] * child
                    linear = linear + node[other] * width[other] * k[other]
                    turns = (turns - jnp.floor(turns)) + linear
                store(level, one, branch, turns)


def level_kernel(layout, x_ref, table_ref, matrix_ref, out_ref, done_ref, sems):
    low_half = lax.broadcasted_iota(jnp.int32, (BLOCK, 128), 1) < 64
    last = len(layout.moved)

    def pack(first, second):
        crossed = pltpu.roll(jnp.where(low_half, second, first), 64, 1)
        return jnp.where(low_half, first, crossed), jnp.where(low_half, crossed, second)

    state = {}
    for one in combos(layout.free(0)):
        halves = []
        for value in range(2):
            first = layout.row({**one, layout.packed[0]: value})
            halves.append(x_ref[first : first + BLOCK, :])
        state[pick(one, layout.free(0))] = pack(*halves)

    for level, moved in enumerate(layout.moved):
        free, packed = layout.free(level), layout.packed[level + 1]
        next_free = layout.free(level + 1)
        matrix = matrix_ref[layout.plan[level][0]]
        later = layout.packed[level + 1 :]
        order = sorted(
            (bit for bit in next_free if bit != moved),
            key=lambda bit: -later.index(bit) if bit in later else -99 * (bit not in layout.packed),
        )
        next_state = {}
        groups = combos(order)
        step = max(1, len(groups) // DOTS)
        for start in range(0, len(groups), step):
            parts = [[], []]
            places = []
            for group in groups[start : start + step]:
                halves = []
                for half in range(2):
                    one = {**group, packed: half}
                    real, imaginary = state[pick(one, free)]
                    turned = []
                    for branch in range(2):
                        cosine, sine = (table_ref[place, :] for place in layout.place(level, one, branch))
                        both = (real * cosine - imaginary * sine, real * sine + imaginary * cosine)
                        turned.append(jnp.concatenate(both, 0))
                    halves.append(turned)
                values = [jnp.concatenate([turned[branch] for turned in halves], 1) for branch in range(2)]
                tops = [value.astype(jnp.bfloat16) for value in values]
                parts[0] += tops
                parts[1] += [
                    (value - top.astype(jnp.float32)).astype(jnp.bfloat16)
                    for value, top in zip(values, tops)
                ]
                places += [pick({**group, moved: branch}, next_free) for branch in range(2)]
            tops = jnp.dot(jnp.concatenate(parts[0], 0), matrix, preferred_element_type=jnp.float32)
            rests = jnp.dot(jnp.concatenate(parts[1], 0), matrix[:, :128], preferred_element_type=jnp.float32)
            for index, place in enumerate(places):
                first = index * 2 * BLOCK
                top, rest = tops[first : first + 2 * BLOCK], rests[first : first + 2 * BLOCK]
                total = (top[:, 128:] + rest) + top[:, :128]
                next_state[place] = (total[:BLOCK], total[BLOCK:])
        state = next_state

    packed, free = layout.packed[last], layout.free(last)
    copies = []
    for one in combos(free):
        real, imaginary = state[pick(one, free)]
        cosine, sine = (table_ref[place, :] for place in layout.place(last, one))
        outputs = pack(real * cosine + imaginary * sine, imaginary * cosine - real * sine)
        for value in range(2):
            first = layout.row({**one, packed: value})
            done_ref[first : first + BLOCK, :] = outputs[value]
        if all(one[bit] == 1 for bit in free[2:]):
            for value in range(2):
                shared = {bit: one[bit] for bit in free[:2]}
                piece = pl.ds(layout.row({**shared, packed: value}), BLOCK << len(free) - 2)
                copy = pltpu.make_async_copy(done_ref.at[piece], out_ref.at[piece], sems.at[len(copies)])
                copy.start()
                copies.append(copy)
    for copy in copies:
        copy.wait()


def rotations(layout):
    vmem = pl.BlockSpec(memory_space=pltpu.VMEM)
    rows = 2 * BLOCK * len(layout.entries)
    return pl.pallas_call(
        functools.partial(table_kernel, layout, ("outer", "inner")),
        out_shape=jax.ShapeDtypeStruct((rows, 128), jnp.float32),
        in_specs=[vmem],
        out_specs=vmem,
        compiler_params=pltpu.CompilerParams(vmem_limit_bytes=VMEM_BYTES),
        cost_estimate=pl.CostEstimate(
            flops=rows * 128 * 20, bytes_accessed=rows * 512, transcendentals=rows * 128
        ),
    )(jnp.asarray(lane_nodes()))


def run_levels(rows, table, layout):
    vmem = pl.BlockSpec(memory_space=pltpu.VMEM)
    return pl.pallas_call(
        functools.partial(level_kernel, layout),
        out_shape=jax.ShapeDtypeStruct(rows.shape, jnp.float32),
        in_specs=[vmem] * 3,
        out_specs=pl.BlockSpec(memory_space=pl.ANY),
        scratch_shapes=[pltpu.VMEM(rows.shape, jnp.float32), pltpu.SemaphoreType.DMA((8,))],
        compiler_params=pltpu.CompilerParams(vmem_limit_bytes=VMEM_BYTES),
    )(rows, table, jnp.asarray(split_matrices()))


def reorder_plan(plan, order):
    def place(bit):
        return bit if bit is None or isinstance(bit, tuple) else order.index(bit)

    return [
        (dimension, place(moved), [[place(b) for b in g] for g in target], [[place(b) for b in g] for g in source])
        for dimension, moved, target, source in plan
    ]


def reorder_rows(rows, order):
    count = len(order)
    if list(order) == list(range(count)):
        return rows
    axes = [count - 1 - order[count - 1 - i] for i in range(count)]
    return rows.reshape((2,) * count + (128,)).transpose(axes + [count]).reshape(rows.shape)


def level_groups(plan, row_bits):
    moved = [entry[1] for entry in plan[:-1]]
    groups = []
    level = 0
    while level < len(moved):
        count = min(len(moved) - level, row_bits - LOW_BITS)
        group = moved[level : level + count]
        order = [bit for bit in range(row_bits) if bit not in group] + sorted(group)
        groups.append((order, Layout(reorder_plan(plan[level : level + count + 1], order), row_bits)))
        level += count
    return groups


def body(weights):
    row_bits = weights.shape[0].bit_length() - 1
    inner_bits = lax.axis_size("inner").bit_length() - 1
    outer_bits = lax.axis_size("outer").bit_length() - 1
    groups = level_groups(level_plan(row_bits, inner_bits, outer_bits), row_bits)
    rows = lax.all_to_all(weights, ("inner", "outer"), 0, 0, tiled=True)
    tables = [rotations(layout) for _, layout in groups]
    for (order, layout), table in zip(groups, tables):
        rows = run_levels(reorder_rows(rows, order), table, layout)
        rows = reorder_rows(rows, [order.index(bit) for bit in range(row_bits)])
    return rows


def solution(mesh):
    spec = P(("outer", "inner"), None)
    return jax.shard_map(body, mesh=mesh, in_specs=(spec,), out_specs=spec, check_vma=False)
```
